512 devices in a mesh: seq: 64 (over z, x), tp: 8 (over y, core).
Axes of the slice: x: 4, y: 4, z: 16, core: 2. Of those that a mesh axis runs over, the one named last changes fastest.
Arguments:
- x_in: bfloat16 [8192, 8192], P('seq', 'tp'), may hold values from -6 to 6
- bc_in: bfloat16 [8192, 2, 2048], P('seq', None, 'tp'), may hold values from -3 to 3
- z_in: bfloat16 [8192, 8192], P('seq', 'tp'), may hold values from -6 to 6
- dt_raw: bfloat16 [8192, 128], P('seq', 'tp'), may hold values from -5 to 5
- starts: int32 [8192], P('seq'), may hold values 0 or 1
- conv_x: float32 [4, 8192], P(None, 'tp'), may hold values from -3 to 3
- conv_bc: float32 [4, 2, 2048], P(None, None, 'tp'), may hold values from -3 to 3
- a_log: float32 [128], P('tp'), may hold values from -9 to -3
- dt_bias: float32 [128], P('tp'), may hold values from -2 to 1
- d_skip: float32 [128], P('tp'), may hold values from 0.5 to 2
- norm_gain: float32 [8192], P('tp'), may hold values from 0.5 to 1.5
Outputs:
- mixed: bfloat16 [8192, 8192], P('seq', 'tp')
The draws below stay inside these ranges and needn't reach their ends.
All inputs are finite; a program needn't handle non-finite values. No bound on the sum of `starts` on one device may be relied on, other than what follows from the above.
Results may differ from the reference program's by a relative error of at most 0.0085.
Values may be sent and summed in bfloat16 or wider, within the bound.
A program may use at most 192 MiB of HBM per device.

```python
import jax
import jax.numpy as jnp
from jax import lax

H_DEV = 16
HEAD_DIM = 64
STATE = 256
CONV = 4
BLOCK = 128
TOK_DEV = 128
HEADS = 128
GROUPS = 8
TOKENS = 8192


def plant(values, rng, smallest, top_value):
    place = [jax.random.randint(jax.random.fold_in(rng, axis), (), 0, length) for axis, length in enumerate(values.shape)]
    longest = values.shape.index(max(values.shape))
    beside = place[:longest] + [(place[longest] + 1) % values.shape[longest]] + place[longest + 1:]
    return values.at[tuple(place)].set(smallest).at[tuple(beside)].set(top_value)


def steps_of(rng, shape, shards, low, largest):
    def one(position, blocks):
        heights = jax.random.uniform(jax.random.fold_in(jax.random.fold_in(rng, 6), position), (blocks,), jnp.float32, low / len(shards), largest / len(shards))
        return jnp.repeat(jnp.exp(heights), shape[position] // blocks).reshape((-1,) + (1,) * (len(shape) - position - 1))

    gain = one(*shards[0])
    for cut in shards[1:]:
        gain = gain * one(*cut)
    return gain


def centred(stream_key, extent, scale, most, cuts=(), kind=jnp.bfloat16):
    drawn = scale * jax.random.normal(stream_key, extent, jnp.float32)
    if cuts:
        drawn = drawn * steps_of(stream_key, extent, cuts, -0.22, 0.18)
    return jnp.clip(drawn, -most, most).astype(kind)


def setup_inputs(seed: int = 0) -> dict:
    seeds = jax.random.split(jax.random.key(seed), 12)
    return {
        "x_in": centred(seeds[0], (TOKENS, HEADS * HEAD_DIM), 1.0, 6.0, ((0, 64), (1, 8))),
        "bc_in": centred(seeds[1], (TOKENS, 2, GROUPS * STATE), 0.5, 3.0, ((0, 64), (2, 8))),
        "z_in": centred(seeds[2], (TOKENS, HEADS * HEAD_DIM), 1.0, 6.0, ((0, 64), (1, 8))),
        "dt_raw": centred(seeds[3], (TOKENS, HEADS), 1.0, 5.0, ((0, 64), (1, 8))),
        "starts": plant((jax.random.randint(seeds[4], (TOKENS,), 0, 16 * TOK_DEV) < 1).astype(jnp.int32), jax.random.fold_in(seeds[4], 1), 0, 1),
        "conv_x": centred(seeds[5], (CONV, HEADS * HEAD_DIM), CONV ** -0.5, 3.0, ((1, 8),), jnp.float32),
        "conv_bc": centred(seeds[6], (CONV, 2, GROUPS * STATE), CONV ** -0.5, 3.0, ((2, 8),), jnp.float32),
        "a_log": jnp.clip(-9.0 + 6.0 * jax.random.uniform(seeds[7], (HEADS,), jnp.float32) ** steps_of(seeds[7], (HEADS,), ((0, 8),), -0.2, 0.2), -9.0, -3.0),
        "dt_bias": jnp.clip(-2.0 + 3.0 * jax.random.uniform(seeds[8], (HEADS,), jnp.float32) ** steps_of(seeds[8], (HEADS,), ((0, 8),), -0.2, 0.2), -2.0, 1.0),
        "d_skip": jnp.clip(0.5 + 1.5 * jax.random.uniform(seeds[9], (HEADS,), jnp.float32) ** steps_of(seeds[9], (HEADS,), ((0, 8),), -0.2, 0.2), 0.5, 2.0),
        "norm_gain": jnp.clip(1.0 + 0.1 * jax.random.normal(seeds[10], (HEADS * HEAD_DIM,), jnp.float32), 0.5, 1.5),
    }


EPSILON = 1e-05

def causal_conv(values, taps, segment):
    count_rows = values.shape[0]
    reach = CONV - 1
    padded = jnp.concatenate([jnp.zeros((reach,) + values.shape[1:], values.dtype), values], 0)
    padded_segment = jnp.concatenate([jnp.zeros((reach,), jnp.int32), segment], 0)
    summed = jnp.zeros(values.shape, jnp.float32)
    for offset in range(CONV):
        shifted = lax.slice_in_dim(padded, reach - offset, reach - offset + count_rows, axis=0).astype(jnp.float32)
        shifted_segment = lax.slice_in_dim(padded_segment, reach - offset, reach - offset + count_rows, axis=0)
        valid_tap = (shifted_segment == segment).astype(jnp.float32)
        valid_tap = valid_tap.reshape((count_rows,) + (1,) * (values.ndim - 1))
        summed = summed + taps[CONV - 1 - offset] * shifted * valid_tap
    return jax.nn.silu(summed).astype(jnp.bfloat16)

def reference(x_in, bc_in, z_in, dt_raw, starts, conv_x, conv_bc, a_log, dt_bias, d_skip, norm_gain):
    segment = jnp.cumsum(starts).astype(jnp.int32)
    x_conv = causal_conv(x_in, conv_x, segment)
    bc_conv = causal_conv(bc_in, conv_bc, segment)
    blocks = TOKENS // BLOCK
    x_blocks = x_conv.reshape(blocks, BLOCK, GROUPS, H_DEV, HEAD_DIM)
    b_blocks = bc_conv[:, 0].reshape(blocks, BLOCK, GROUPS, STATE)
    c_blocks = bc_conv[:, 1].reshape(blocks, BLOCK, GROUPS, STATE)
    step_size = jax.nn.softplus(dt_raw.astype(jnp.float32) + dt_bias[None, :])
    log_decay = step_size * (-jnp.exp(a_log))[None, :]
    step_blocks = step_size.reshape(blocks, BLOCK, GROUPS, H_DEV)
    decay_blocks = log_decay.reshape(blocks, BLOCK, GROUPS, H_DEV)
    start_blocks = starts.reshape(blocks, BLOCK)
    causal = jnp.arange(BLOCK)[:, None] >= jnp.arange(BLOCK)[None, :]

    def one_block(state_now, inputs):
        x_blk, b_blk, c_blk, step_blk, decay_blk, start_blk = inputs
        cumulative = jnp.cumsum(decay_blk, axis=0)
        inner_seg = jnp.cumsum(start_blk).astype(jnp.int32)
        linked = causal & (inner_seg[:, None] == inner_seg[None, :])
        scores = jnp.einsum('ign,jgn->gij', c_blk.astype(jnp.float32), b_blk.astype(jnp.float32))
        cum_heads = cumulative.transpose(1, 2, 0)
        log_gap = cum_heads[:, :, :, None] - cum_heads[:, :, None, :]
        mixing = jnp.where(linked[None, None], jnp.exp(jnp.minimum(log_gap, 0.0)), 0.0)
        mixing = mixing * scores[:, None] * step_blk.transpose(1, 2, 0)[:, :, None, :]
        mixing = mixing.astype(jnp.bfloat16)
        y_intra = jnp.einsum('ghij,jghp->ighp', mixing.astype(jnp.float32), x_blk.astype(jnp.float32))
        enter_factor = jnp.exp(cumulative) * (inner_seg == 0).astype(jnp.float32)[:, None, None]
        y_state = enter_factor[..., None] * jnp.einsum('ign,ghpn->ighp', c_blk.astype(jnp.float32), state_now, precision=lax.Precision.HIGHEST)
        last_log = cumulative[-1]
        tail_linked = (inner_seg == inner_seg[-1]).astype(jnp.float32)
        coefficient = jnp.exp(last_log[None] - cumulative) * step_blk * tail_linked[:, None, None]
        weighted = (x_blk.astype(jnp.float32) * coefficient[..., None]).astype(jnp.bfloat16)
        block_state = jnp.einsum('jghp,jgn->ghpn', weighted.astype(jnp.float32), b_blk.astype(jnp.float32))
        carried = jnp.exp(last_log) * (inner_seg[-1] == 0).astype(jnp.float32)
        next_state = carried[..., None, None] * state_now + block_state
        return (next_state, y_intra + y_state)
    empty_state = jnp.zeros((GROUPS, H_DEV, HEAD_DIM, STATE), jnp.float32)
    final_state, outputs = lax.scan(one_block, empty_state, (x_blocks, b_blocks, c_blocks, step_blocks, decay_blocks, start_blocks))
    y_total = outputs.reshape(TOKENS, HEADS, HEAD_DIM)
    y_total = y_total + d_skip[None, :, None] * x_conv.reshape(TOKENS, HEADS, HEAD_DIM).astype(jnp.float32)
    gated_out = y_total * jax.nn.silu(z_in.reshape(TOKENS, HEADS, HEAD_DIM).astype(jnp.float32))
    mean_square = lax.optimization_barrier(jnp.mean(gated_out * gated_out, axis=(1, 2)))
    inverse_rms = lax.rsqrt(mean_square + EPSILON)
    result = gated_out * inverse_rms[:, None, None] * norm_gain.reshape(HEADS, HEAD_DIM)[None]
    return result.reshape(TOKENS, HEADS * HEAD_DIM).astype(jnp.bfloat16)
```

```python
import functools

import jax
import jax.numpy as jnp
from jax import lax
from jax.experimental import pallas as pl
from jax.experimental.pallas import tpu as pltpu
from jax.sharding import PartitionSpec as P

NX = 4
CHUNKS = 2
HALO = 16
REACH = 3
EPSILON = 1e-05
MESH = pl.DeviceIdType.MESH
F32, BF16 = jnp.float32, jnp.bfloat16


def dot(a, b):
    return jnp.dot(a, b, preferred_element_type=F32)


def dot_nt(a, b):
    return lax.dot_general(a, b, (((1,), (1,)), ((), ())), preferred_element_type=F32)


def dot_tn(a, b):
    return lax.dot_general(a, b, (((0,), (0,)), ((), ())), preferred_element_type=F32)


def iota(shape, axis):
    return lax.broadcasted_iota(jnp.int32, shape, axis)


def pieces(value, count):
    parts = []
    for _ in range(count):
        part = value.astype(BF16)
        parts.append(part)
        value = value - part.astype(F32)
    return jnp.concatenate(parts, axis=0)


def kernel(
    nz, nx, ntp,
    x_ref, bc_ref, z_ref, dt_ref, st_ref, cx_ref, cbc_ref, al_ref, db_ref, ds_ref, ng_ref,
    out_ref,
    xext, hsend, xc, crecv, dsend, drecv, tot_send, tot_recv,
    sbuf, srecv, lbuf, ylbuf, tbuf, zrecv, obuf, szbuf, ysend, yrecv,
    ebuf, yi, sz, gbuf, ssend, ssrecv,
    h_sem, d_sem, t_sem, c_sem, s_sem, zf_sem, zb_sem, y_sem, n_sem,
):
    seq, tp = lax.axis_index("seq"), lax.axis_index("tp")
    mz, mx = seq // nx, seq % nx
    nseq = nz * nx
    rows, channels = x_ref.shape
    state = bc_ref.shape[1] // 2
    heads = dt_ref.shape[0]
    quarter = channels // nx
    width = quarter // CHUNKS
    wide = HALO + rows

    def x_peer(r):
        q = (mx + r) % nx
        return q, {"seq": mz * nx + q}

    def z_peer(r):
        k = (mz + r) % nz
        return k, {"seq": k * nx + mx}

    def t_peer(r):
        return {"tp": (tp + r) % ntp}

    following, preceding = {"seq": (seq + 1) % nseq}, {"seq": (seq + nseq - 1) % nseq}

    def remote(src, dst, sem, device):
        return pltpu.make_async_remote_copy(
            src_ref=src, dst_ref=dst, send_sem=sem.at[0], recv_sem=sem.at[1],
            device_id=device, device_id_type=MESH,
        )

    barrier = pltpu.get_barrier_semaphore()

    def greet(device):
        pl.semaphore_signal(barrier, inc=1, device_id=device, device_id_type=MESH)

    greet(following)
    greet(preceding)
    for r in range(1, nx):
        greet(x_peer(r)[1])

    @pl.loop(1, nz)
    def _(r):
        greet(z_peer(r)[1])

    for r in range(1, ntp):
        greet(t_peer(r))

    starts = st_ref[...].astype(F32)
    starts_wide = jnp.broadcast_to(starts, (wide, rows)).astype(BF16)
    row, col = iota((rows, rows), 0), iota((rows, rows), 1)
    tril = (col <= row).astype(F32).astype(BF16)
    ranges = [tril, (col > row).astype(F32).astype(BF16)]
    for d in range(1, REACH + 1):
        ranges.append(((col <= row) & (col > row - d)).astype(F32).astype(BF16))
    counts = dot_nt(jnp.concatenate(ranges, axis=0), starts_wide)
    seg_col = counts[:rows, :rows]
    to_last = (counts[rows : 2 * rows, :rows] == 0.0).astype(F32)
    seg_row = dot_nt(starts_wide[:rows], tril)
    linked = (seg_col == seg_row) & (col <= row)
    from_first = (seg_col == 0.0).astype(F32)
    tap_row, tap_col = iota((rows, wide), 0), iota((rows, wide), 1)
    first_col = jnp.where(seq == 0, HALO, 0)
    taps = []
    for d in range(1, REACH + 1):
        none_between = counts[(d + 1) * rows : (d + 2) * rows] == 0.0
        place = (tap_col - HALO == tap_row - d) & (tap_col >= first_col)
        taps.append((place & none_between).astype(F32).astype(BF16))
    taps = jnp.concatenate(taps, axis=0)

    xext[HALO:, :channels] = x_ref[...]
    xext[HALO:, channels:] = bc_ref[...]
    keep = to_last[rows - HALO :, :1]
    hsend[...] = (xext[rows:, :].astype(F32) * keep).astype(BF16)

    raw = dt_ref[...].astype(F32) + db_ref[...]
    step = jnp.maximum(raw, 0.0) + jnp.log1p(jnp.exp(-jnp.abs(raw)))
    decay = -jnp.exp(al_ref[...]) * step
    parts = dot_nt(pieces(decay, 3), tril)
    cumulative = parts[:heads] + parts[heads : 2 * heads] + parts[2 * heads :]
    spread = (iota((heads, channels), 1) // (channels // heads) == iota((heads, channels), 0))
    spread = spread.astype(F32).astype(BF16)
    spread2 = jnp.concatenate([spread, spread], axis=0)
    ebuf[...] = dot_tn(pieces(jnp.exp(cumulative), 2), spread2)
    fall = ebuf[rows - 1 :, :]
    whole = (counts[rows - 1 : rows, :1] == 0.0).astype(F32)
    through = fall * whole
    for q in range(nx):
        for c in range(CHUNKS):
            at = q * quarter + c * width
            dsend[q, c : c + 1, :] = through[:, at : at + width]

    pl.semaphore_wait(barrier, (nx - 1) + (nz - 1) + (ntp - 1) + 2)

    halo = remote(hsend, xext.at[pl.ds(0, HALO)], h_sem, following)
    halo.start()
    for r in range(1, nx):
        q, device = x_peer(r)
        remote(dsend.at[q], drecv.at[mx], d_sem, device).start()
    drecv[mx] = dsend[mx]

    factor = dot_tn(pieces(jnp.exp(-cumulative) * step, 2), spread2)
    halo.wait_recv()

    def conv(at, size, weights):
        block = xext[:, at : at + size]
        shifted = dot(taps, block)
        total = weights[REACH] * block[HALO:].astype(F32)
        for d in range(1, REACH + 1):
            total += weights[REACH - d] * shifted[(d - 1) * rows : d * rows]
        return total * jax.nn.sigmoid(total)

    b = conv(channels, state, [cbc_ref[k, 0:1, :] for k in range(REACH + 1)])
    b = b.astype(BF16)
    bt = jnp.transpose(b.astype(F32) * to_last[:, :1]).astype(BF16)
    cc = conv(channels + state, state, [cbc_ref[k, 1:2, :] for k in range(REACH + 1)])
    cc = cc.astype(BF16)
    crecv[mx] = cc
    for r in range(1, nx):
        _, device = x_peer(r)
    fx = []
    for q in range(nx):
        at = q * quarter
        piece = conv(at, quarter, [cx_ref[k : k + 1, at : at + quarter] for k in range(REACH + 1)])
        piece = piece.astype(BF16)
        xc[:, at : at + quarter] = piece
        fx.append((piece.astype(F32) * factor[:, at : at + quarter]).astype(BF16))

    for c in range(CHUNKS):
        for q in range(nx):
            at = q * quarter + c * width
            made = dot(bt, fx[q][:, c * width : (c + 1) * width])
            sbuf[c, q] = (made * fall[:, at : at + width]).astype(BF16)
        for r in range(1, nx):
            q, device = x_peer(r)
            remote(sbuf.at[c, q], srecv.at[c, mx], s_sem.at[c], device).start()
        srecv[c, mx] = sbuf[c, mx]
    for r in range(1, nx):
        _, device = x_peer(r)
        remote(crecv.at[mx], crecv.at[mx], c_sem, device).start()

    def await_recv(buffer, count, sem):
        part = buffer.at[pl.ds(0, count)]
        remote(part, part, sem, following).wait_recv()

    def await_send(buffer, count, sem):
        part = buffer.at[pl.ds(0, count)]
        remote(part, part, sem, following).wait_send()

    await_recv(drecv, nx - 1, d_sem)
    reach_of = [None, drecv[0]]
    for k in range(1, nx):
        reach_of.append(reach_of[-1] * drecv[k])
    tot_send[...] = reach_of[nx]
    tot_recv[mz] = reach_of[nx]

    @pl.loop(1, nz)
    def _(r):
        k, device = z_peer(r)
        remote(tot_send, tot_recv.at[mz], t_sem, device).start()

    scores = jnp.where(linked, dot_nt(cc, b), 0.0).astype(BF16)
    for q in range(nx):
        at = q * quarter
        yi[:, at : at + quarter] = dot(scores, fx[q])
    gate = z_ref[...].astype(F32)
    sz[...] = gate * jax.nn.sigmoid(gate)

    for c in range(CHUNKS):
        await_recv(srecv.at[c], nx - 1, s_sem.at[c])
        running = srecv[c, 0].astype(F32)
        for k in range(1, nx):
            lbuf[c, k - 1] = running.astype(BF16)
            running = drecv[k, c : c + 1, :] * running + srecv[c, k].astype(F32)
        tbuf[c] = running.astype(BF16).reshape(nz, state // nz, width)
        zrecv[c, mz] = tbuf[c, mz]

        @pl.loop(1, nz)
        def _(r):
            k, device = z_peer(r)
            remote(tbuf.at[c, k], zrecv.at[c, mz], zf_sem.at[c], device).start()

    await_recv(crecv, nx - 1, c_sem)
    for c in range(CHUNKS):
        for k in range(1, nx):
            ylbuf[c, k - 1] = dot(crecv[k], lbuf[c, k - 1])

    await_recv(tot_recv, nz - 1, t_sem)
    for c in range(CHUNKS):
        await_recv(zrecv.at[c], nz - 1, zf_sem.at[c])
        running = jnp.zeros((state // nz, width), F32)
        for k in range(nz):
            obuf[c, k] = running.astype(BF16)
            running = tot_recv[k, c : c + 1, :] * running + zrecv[c, k].astype(F32)
        szbuf[c, mz] = obuf[c, mz]

        @pl.loop(1, nz)
        def _(r):
            k, device = z_peer(r)
            remote(obuf.at[c, k], szbuf.at[c, mz], zb_sem.at[c], device).start()

    for c in range(CHUNKS):
        await_recv(szbuf.at[c], nz - 1, zb_sem.at[c])
        entering = szbuf[c].reshape(state, width)
        for k in range(nx):
            part = dot(crecv[k], entering)
            if k:
                part = reach_of[k][c : c + 1, :] * part + ylbuf[c, k - 1]
            ysend[c, k] = part.astype(BF16)
        yrecv[c, mx] = ysend[c, mx]
        for r in range(1, nx):
            q, device = x_peer(r)
            remote(ysend.at[c, q], yrecv.at[c, mx], y_sem.at[c], device).start()

    skip = dot_tn(pieces(jnp.broadcast_to(ds_ref[...], (heads, 128)), 2), spread2)[:1]
    squares = jnp.zeros((rows, 128), F32)
    for c in range(CHUNKS):
        await_recv(yrecv.at[c], nx - 1, y_sem.at[c])
        for q in range(nx):
            at = slice(q * quarter + c * width, q * quarter + (c + 1) * width)
            y = yi[:, at] + from_first[:, :1] * yrecv[c, q].astype(F32)
            y = ebuf[:, at] * y + skip[:, at] * xc[:, at].astype(F32)
            gated = y * sz[:, at]
            gbuf[:, at] = gated
            for k in range(0, width, 128):
                part = gated[:, k : k + 128]
                squares += part * part
    total = jnp.sum(jnp.transpose(squares), axis=0, keepdims=True)
    total = jnp.broadcast_to(total, ssend.shape)
    ssend[...] = total
    ssrecv[tp] = total
    for r in range(1, ntp):
        remote(ssend, ssrecv.at[tp], n_sem, t_peer(r)).start()
    await_recv(ssrecv, ntp - 1, n_sem)
    total = jnp.sum(ssrecv[...], axis=0)[:1]
    inverse = lax.rsqrt(total / (channels * ntp) + EPSILON)
    inverse = jnp.transpose(jnp.broadcast_to(inverse, (rows, rows)))
    for at in range(0, channels, 128):
        at = slice(at, at + 128)
        out_ref[:, at] = (gbuf[:, at] * inverse * ng_ref[:, at]).astype(BF16)

    halo.wait_send()
    await_send(drecv, nx - 1, d_sem)
    await_send(tot_recv, nz - 1, t_sem)
    await_send(crecv, nx - 1, c_sem)
    for c in range(CHUNKS):
        await_send(srecv.at[c], nx - 1, s_sem.at[c])
        await_send(zrecv.at[c], nz - 1, zf_sem.at[c])
        await_send(szbuf.at[c], nz - 1, zb_sem.at[c])
        await_send(yrecv.at[c], nx - 1, y_sem.at[c])
    await_send(ssrecv, ntp - 1, n_sem)


def per_device(
    x_in, bc_in, z_in, dt_raw, starts, conv_x, conv_bc, a_log, dt_bias, d_skip, norm_gain
):
    rows, channels = x_in.shape
    state = bc_in.shape[2]
    heads = dt_raw.shape[1]
    nx, ntp = NX, lax.axis_size("tp")
    nz = lax.axis_size("seq") // nx
    width = channels // nx // CHUNKS
    vmem = pl.BlockSpec(memory_space=pltpu.VMEM)
    sems = pltpu.SemaphoreType.DMA
    return pl.pallas_call(
        functools.partial(kernel, nz, nx, ntp),
        out_shape=jax.ShapeDtypeStruct((rows, channels), BF16),
        in_specs=[vmem] * 11,
        out_specs=vmem,
        scratch_shapes=[
            pltpu.VMEM((HALO + rows, channels + 2 * state), BF16),
            pltpu.VMEM((HALO, channels + 2 * state), BF16),
            pltpu.VMEM((rows, channels), BF16),
            pltpu.VMEM((nx, rows, state), BF16),
            pltpu.VMEM((nx, CHUNKS, width), F32),
            pltpu.VMEM((nx, CHUNKS, width), F32),
            pltpu.VMEM((CHUNKS, width), F32),
            pltpu.VMEM((nz, CHUNKS, width), F32),
            pltpu.VMEM((CHUNKS, nx, state, width), BF16),
            pltpu.VMEM((CHUNKS, nx, state, width), BF16),
            pltpu.VMEM((CHUNKS, nx - 1, state, width), BF16),
            pltpu.VMEM((CHUNKS, nx - 1, rows, width), F32),
            pltpu.VMEM((CHUNKS, nz, state // nz, width), BF16),
            pltpu.VMEM((CHUNKS, nz, state // nz, width), BF16),
            pltpu.VMEM((CHUNKS, nz, state // nz, width), BF16),
            pltpu.VMEM((CHUNKS, nz, state // nz, width), BF16),
            pltpu.VMEM((CHUNKS, nx, rows, width), BF16),
            pltpu.VMEM((CHUNKS, nx, rows, width), BF16),
            pltpu.VMEM((rows, channels), F32),
            pltpu.VMEM((rows, channels), F32),
            pltpu.VMEM((rows, channels), F32),
            pltpu.VMEM((rows, channels), F32),
            pltpu.VMEM((8, 128), F32),
            pltpu.VMEM((ntp, 8, 128), F32),
            sems((2,)),
            sems((2,)),
            sems((2,)),
            sems((2,)),
            sems((CHUNKS, 2)),
            sems((CHUNKS, 2)),
            sems((CHUNKS, 2)),
            sems((CHUNKS, 2)),
            sems((2,)),
        ],
        compiler_params=pltpu.CompilerParams(
            collective_id=0, has_side_effects=True, vmem_limit_bytes=32 * 2**20
        ),
        cost_estimate=pl.CostEstimate(flops=2 * 10**8, bytes_accessed=2**20, transcendentals=10**6),
    )(
        x_in,
        bc_in.reshape(rows, 2 * state),
        z_in,
        dt_raw.T,
        starts.reshape(1, rows),
        conv_x,
        conv_bc,
        a_log.reshape(heads, 1),
        dt_bias.reshape(heads, 1),
        d_skip.reshape(heads, 1),
        norm_gain.reshape(1, channels),
    )


def solution(mesh):
    return jax.shard_map(
        per_device,
        mesh=mesh,
        in_specs=(
            P("seq", "tp"),
            P("seq", None, "tp"),
            P("seq", "tp"),
            P("seq", "tp"),
            P("seq"),
            P(None, "tp"),
            P(None, None, "tp"),
            P("tp"),
            P("tp"),
            P("tp"),
            P("tp"),
        ),
        out_specs=P("seq", "tp"),
        check_vma=False,
    )
```

```python
import functools

import jax
import jax.numpy as jnp
from jax import lax
from jax.experimental import pallas as pl
from jax.experimental.pallas import tpu as pltpu
from jax.sharding import PartitionSpec as P

NX = 4
GROUP = 4
CHUNKS = 2
HEAD = 16
REACH = 3
FOLD = 4
EPSILON = 1e-05
MESH = pl.DeviceIdType.MESH
F32, BF16 = jnp.float32, jnp.bfloat16


def dot(a, b):
    return jnp.dot(a, b, preferred_element_type=F32)


def dot_nt(a, b):
    return lax.dot_general(a, b, (((1,), (1,)), ((), ())), preferred_element_type=F32)


def dot_tn(a, b):
    return lax.dot_general(a, b, (((0,), (0,)), ((), ())), preferred_element_type=F32)


def iota(shape, axis):
    return lax.broadcasted_iota(jnp.int32, shape, axis)


def pieces(value, count):
    parts = []
    for _ in range(count):
        part = value.astype(BF16)
        parts.append(part)
        value = value - part.astype(F32)
    return jnp.concatenate(parts, axis=0)


def silu(value):
    return value * jax.nn.sigmoid(value)


def kernel(
    nz, nx, ntp,
    x_hbm, bc_hbm, z_hbm, dt_hbm, st_hbm, cx_hbm, cbc_hbm, al_hbm, db_hbm, ds_hbm, ng_hbm,
    out_ref,
    x_ref, bc_ref, z_ref, dt_ref, st_ref, cx_ref, cbc_ref, al_ref, db_ref, ds_ref, ng_ref,
    hsend, hrecv, pre, weights, xc, fx, bcv, crecv, dsend, drecv, tot_send, tot_recv,
    sbuf, srecv, lbuf, ylbuf, tbuf, zrecv, prebuf, pout, pin, obuf, szbuf, ysend, yrecv,
    ebuf, yi, sz, gbuf, ssend, ssrecv,
    in_sem, h_sem, d_sem, t_sem, c_sem, s_sem, zf_sem, p_sem, zb_sem, y_sem, n_sem, near_sem,
):
    seq, tp = lax.axis_index("seq"), lax.axis_index("tp")
    mz, mx = seq // nx, seq % nx
    nseq, ngroups = nz * nx, nz // GROUP
    group, member = mz // GROUP, mz % GROUP
    rows, channels = x_ref.shape
    state = bc_ref.shape[2]
    heads = dt_ref.shape[0]
    quarter = channels // nx
    width = quarter // CHUNKS
    total_width = channels + 2 * state
    part = state // GROUP

    def seq_at(z, x):
        return {"seq": z * nx + x}

    def x_peer(r):
        q = (mx + r) % nx
        return q, seq_at(mz, q)

    def z_peer(r):
        k = (member + r) % GROUP
        return k, seq_at(group * GROUP + k, mx)

    def t_peer(r):
        return {"tp": (tp + r) % ntp}

    following, preceding = {"seq": seq + 1}, {"seq": seq - 1}
    next_group = seq_at(mz + GROUP, mx)

    def remote(src, dst, sem, device):
        return pltpu.make_async_remote_copy(
            src_ref=src, dst_ref=dst, send_sem=sem.at[0], recv_sem=sem.at[1],
            device_id=device, device_id_type=MESH,
        )

    def await_recv(buffer, count, sem):
        some = buffer.at[pl.ds(0, count)]
        remote(some, some, sem, x_peer(1)[1]).wait_recv()

    def await_send(buffer, count, sem):
        some = buffer.at[pl.ds(0, count)]
        remote(some, some, sem, x_peer(1)[1]).wait_send()

    loads = [
        pltpu.make_async_copy(src, dst, in_sem.at[k])
        for k, (src, dst) in enumerate([
            (st_hbm, st_ref), (dt_hbm, dt_ref), (al_hbm, al_ref), (db_hbm, db_ref),
            (x_hbm, x_ref), (bc_hbm, bc_ref), (cx_hbm, cx_ref), (cbc_hbm, cbc_ref),
            (z_hbm, z_ref), (ds_hbm, ds_ref), (ng_hbm, ng_ref),
        ])
    ]
    for load in loads:
        load.start()

    barrier = pltpu.get_barrier_semaphore()

    def greet(device, sem=barrier):
        pl.semaphore_signal(sem, inc=1, device_id=device, device_id_type=MESH)

    def greet_along_z(distance, sem):
        @pl.when(mz >= distance)
        def _():
            greet(seq_at(mz - distance, mx), sem)

        @pl.when(mz + distance < nz)
        def _():
            greet(seq_at(mz + distance, mx), sem)

    def both(distance):
        return (mz >= distance).astype(jnp.int32) + (mz + distance < nz).astype(jnp.int32)

    for r in range(1, nx):
        greet(x_peer(r)[1])
    for r in range(2, GROUP):
        @pl.when(member >= r)
        def _():
            greet(seq_at(mz - r, mx))

        @pl.when(member + r < GROUP)
        def _():
            greet(seq_at(mz + r, mx))

    greet_along_z(1, barrier)

    @pl.when(seq > 0)
    def _():
        greet(preceding)

    for r in range(1, ntp):
        greet(t_peer(r))
    greeted = (nx - 1) + (ntp - 1) + both(1) + (seq + 1 < nseq).astype(jnp.int32)
    for r in range(2, GROUP):
        greeted += (member >= r).astype(jnp.int32) + (member + r < GROUP).astype(jnp.int32)

    row, col = iota((rows, rows), 0), iota((rows, rows), 1)
    tril = (col <= row).astype(F32).astype(BF16)
    ranges = [tril, (col > row).astype(F32).astype(BF16)]
    for d in range(1, REACH + 1):
        ranges.append(((col <= row) & (col > row - d)).astype(F32).astype(BF16))
    spread = iota((heads, channels), 1) // (channels // heads) == iota((heads, channels), 0)
    spread = spread.astype(F32).astype(BF16)
    spread2 = jnp.concatenate([spread, spread], axis=0)
    for load in loads[:4]:
        load.wait()
    starts = jnp.broadcast_to(st_ref[...].astype(F32), (rows, rows)).astype(BF16)
    counts = dot_nt(jnp.concatenate(ranges, axis=0), starts)
    seg_col = counts[:rows]
    to_last = (counts[rows : 2 * rows] == 0.0).astype(F32)
    linked = (seg_col == dot_nt(starts, tril)) & (col <= row)
    from_first = (seg_col == 0.0).astype(F32)
    none_between = [counts[(d + 1) * rows : (d + 2) * rows] == 0.0 for d in range(1, REACH + 1)]
    taps = jnp.concatenate(
        [((col == row - d) & none_between[d - 1]).astype(F32).astype(BF16) for d in range(1, REACH + 1)],
        axis=0,
    )

    for load in loads[4:8]:
        load.wait()
    weights[:, :channels] = cx_ref[...]
    for k in range(REACH + 1):
        weights[k : k + 1, channels : channels + state] = cbc_ref[k, 0:1, :]
        weights[k : k + 1, channels + state :] = cbc_ref[k, 1:2, :]
    b_in, c_in = bc_ref[:, 0, :], bc_ref[:, 1, :]

    tail = slice(rows - 8, rows)
    last_rows = jnp.concatenate(
        [x_ref[tail, :].astype(F32), b_in[tail].astype(F32), c_in[tail].astype(F32)], axis=1
    )
    last_rows = (last_rows * to_last[tail, :1])[8 - FOLD :]
    piece = total_width // FOLD
    hsend[...] = jnp.concatenate(
        [last_rows[:, k * piece : (k + 1) * piece] for k in range(FOLD)], axis=0
    ).astype(BF16)

    def column(ref):
        square = (heads, heads)
        here = iota(square, 0) == iota(square, 1)
        return jnp.sum(jnp.where(here, jnp.broadcast_to(ref[...], square), 0.0), axis=1, keepdims=True)

    raw = dt_ref[...].astype(F32) + column(db_ref)
    step = jnp.maximum(raw, 0.0) + jnp.log1p(jnp.exp(-jnp.abs(raw)))
    decay = -jnp.exp(column(al_ref)) * step
    parts = dot_nt(pieces(decay, 3), tril)
    cumulative = parts[:heads] + parts[heads : 2 * heads] + parts[2 * heads :]
    ebuf[...] = dot_tn(pieces(jnp.exp(cumulative), 2), spread2)
    fall = ebuf[rows - 1 :, :]
    through = fall * (seg_col[rows - 1 : rows, :1] == 0.0).astype(F32)
    for q in range(nx):
        for c in range(CHUNKS):
            at = q * quarter + c * width
            dsend[q, c : c + 1, :] = through[:, at : at + width]
    factor = dot_tn(pieces(jnp.exp(-cumulative) * step, 2), spread2)

    def conv(values, at):
        size = values.shape[1]
        taken = weights[:, at : at + size]
        shifted = dot(taps, values)
        total = taken[REACH:] * values.astype(F32)
        for d in range(1, REACH + 1):
            total += taken[REACH - d : REACH - d + 1] * shifted[(d - 1) * rows : d * rows]
        pre[:, at : at + size] = total[:HEAD]
        return silu(total)

    bcv[:, :state] = conv(b_in, channels).astype(BF16)
    bcv[:, state:] = conv(c_in, channels + state).astype(BF16)
    for at in range(0, channels, 256):
        xc[:, at : at + 256] = conv(x_ref[:, at : at + 256], at).astype(BF16)

    pl.semaphore_wait(barrier, greeted)

    halo = remote(hsend, hrecv, h_sem, following)

    @pl.when(seq + 1 < nseq)
    def _():
        halo.start()

    greet_along_z(1, near_sem.at[0])
    for r in range(1, nx):
        q, device = x_peer(r)
        remote(dsend.at[q], drecv.at[mx], d_sem, device).start()
    drecv[mx] = dsend[mx]
    for at in range(0, channels, 256):
        at = slice(at, at + 256)
        fx[HEAD:, at] = (xc[HEAD:, at].astype(F32) * factor[HEAD:, at]).astype(BF16)

    @pl.when(seq == 0)
    def _():
        hrecv[...] = jnp.zeros(hrecv.shape, BF16)

    @pl.when(seq > 0)
    def _():
        halo.wait_recv()

    place_row, place_col = iota((HEAD, HEAD), 0), iota((HEAD, HEAD), 1)
    for k in range(FOLD):
        at = slice(k * piece, (k + 1) * piece)
        reached = []
        for d in range(1, REACH + 1):
            here = (place_col - (k + 1) * FOLD == place_row - d) & (place_row < d)
            here &= none_between[d - 1][:HEAD, :HEAD] & (place_col >= k * FOLD)
            reached.append(here.astype(F32).astype(BF16))
        added = dot(jnp.concatenate(reached, axis=0), hrecv[...])
        total = pre[:, at]
        for d in range(1, REACH + 1):
            total += weights[REACH - d : REACH - d + 1, at] * added[(d - 1) * HEAD : d * HEAD]
        pre[:, at] = total
    done = silu(pre[...]).astype(BF16)
    xc[:HEAD, :] = done[:, :channels]
    bcv[:HEAD, :] = done[:, channels:]
    fx[:HEAD, :] = (done[:, :channels].astype(F32) * factor[:HEAD]).astype(BF16)
    b = bcv[:, :state]
    bt = jnp.transpose(b.astype(F32) * to_last[:, :1]).astype(BF16)

    for c in range(CHUNKS):
        for q in range(nx):
            at = slice(q * quarter + c * width, q * quarter + (c + 1) * width)
            sbuf[c, q] = (dot(bt, fx[:, at]) * fall[:, at]).astype(BF16)
        for r in range(1, nx):
            q, device = x_peer(r)
            remote(sbuf.at[c, q], srecv.at[c, mx], s_sem.at[c], device).start()
        srecv[c, mx] = sbuf[c, mx]
    cc = bcv[:, state:]
    crecv[mx] = cc
    for r in range(1, nx):
        _, device = x_peer(r)
        remote(crecv.at[mx], crecv.at[mx], c_sem, device).start()

    await_recv(drecv, nx - 1, d_sem)
    reach_of = [None, drecv[0]]
    for k in range(1, nx):
        reach_of.append(reach_of[-1] * drecv[k])
    tot_send[...] = reach_of[nx]
    tot_recv[member] = reach_of[nx]
    for r in range(1, GROUP):
        k, device = z_peer(r)
        remote(tot_send, tot_recv.at[member], t_sem, device).start()
    pl.semaphore_wait(near_sem.at[0], both(1))
    if GROUP > 2:
        greet_along_z(2, near_sem.at[1])

    scores = jnp.where(linked, dot_nt(cc, b), 0.0).astype(BF16)
    for q in range(nx):
        at = slice(q * quarter, (q + 1) * quarter)
        yi[:, at] = dot(scores, fx[:, at])
    for load in loads[8:]:
        load.wait()
    sz[...] = silu(z_ref[...].astype(F32))

    for c in range(CHUNKS):
        await_recv(srecv.at[c], nx - 1, s_sem.at[c])
        running = srecv[c, 0].astype(F32)
        for k in range(1, nx):
            lbuf[c, k - 1] = running.astype(BF16)
            running = drecv[k, c : c + 1, :] * running + srecv[c, k].astype(F32)
        tbuf[c] = running.astype(BF16).reshape(GROUP, part, width)
        zrecv[c, member] = tbuf[c, member]
        for r in range(1, GROUP):
            k, device = z_peer(r)
            remote(tbuf.at[c, k], zrecv.at[c, member], zf_sem.at[c], device).start()

    await_recv(crecv, nx - 1, c_sem)
    for c in range(CHUNKS):
        for k in range(1, nx):
            ylbuf[c, k - 1] = dot(crecv[k], lbuf[c, k - 1])

    if GROUP > 2:
        pl.semaphore_wait(near_sem.at[1], both(2))
    await_recv(tot_recv, GROUP - 1, t_sem)
    row_fall = [tot_recv[k] for k in range(GROUP)]
    for c in range(CHUNKS):
        await_recv(zrecv.at[c], GROUP - 1, zf_sem.at[c])
        running = zrecv[c, 0].astype(F32)
        reach = row_fall[0][c : c + 1]
        for k in range(1, GROUP):
            prebuf[c, k] = running
            running = row_fall[k][c : c + 1] * running + zrecv[c, k].astype(F32)
            reach = row_fall[k][c : c + 1] * reach

        @pl.when(group == 0)
        def _():
            pin[c] = jnp.zeros(pin.shape[1:], BF16)

        @pl.when(group > 0)
        def _():
            remote(pout.at[c], pin.at[c], p_sem.at[c], next_group).wait_recv()

        before = pin[c].astype(F32)

        @pl.when(group + 1 < ngroups)
        def _():
            pout[c] = (reach * before + running).astype(BF16)
            remote(pout.at[c], pin.at[c], p_sem.at[c], next_group).start()

        obuf[c, 0] = pin[c]
        reach = row_fall[0][c : c + 1]
        for k in range(1, GROUP):
            obuf[c, k] = (reach * before + prebuf[c, k]).astype(BF16)
            reach = row_fall[k][c : c + 1] * reach
        szbuf[c, member] = obuf[c, member]
        for r in range(1, GROUP):
            k, device = z_peer(r)
            remote(obuf.at[c, k], szbuf.at[c, member], zb_sem.at[c], device).start()

    for c in range(CHUNKS):
        await_recv(szbuf.at[c], GROUP - 1, zb_sem.at[c])
        entering = szbuf[c].reshape(state, width)
        for k in range(nx):
            part_y = dot(crecv[k], entering)
            if k:
                part_y = reach_of[k][c : c + 1, :] * part_y + ylbuf[c, k - 1]
            ysend[c, k] = part_y.astype(BF16)
        yrecv[c, mx] = ysend[c, mx]
        for r in range(1, nx):
            q, device = x_peer(r)
            remote(ysend.at[c, q], yrecv.at[c, mx], y_sem.at[c], device).start()

    skip = dot_tn(pieces(jnp.broadcast_to(column(ds_ref), (heads, 128)), 2), spread2)[:1]
    squares = jnp.zeros((rows, 128), F32)
    for c in range(CHUNKS):
        await_recv(yrecv.at[c], nx - 1, y_sem.at[c])
        for q in range(nx):
            at = slice(q * quarter + c * width, q * quarter + (c + 1) * width)
            y = yi[:, at] + from_first[:, :1] * yrecv[c, q].astype(F32)
            y = ebuf[:, at] * y + skip[:, at] * xc[:, at].astype(F32)
            gated = y * sz[:, at]
            gbuf[:, at] = gated
            for k in range(0, width, 128):
                some = gated[:, k : k + 128]
                squares += some * some
    total = jnp.sum(jnp.transpose(squares), axis=0, keepdims=True)
    total = jnp.broadcast_to(total, ssend.shape)
    ssend[...] = total
    ssrecv[tp] = total
    for r in range(1, ntp):
        remote(ssend, ssrecv.at[tp], n_sem, t_peer(r)).start()
    await_recv(ssrecv, ntp - 1, n_sem)
    total = jnp.sum(ssrecv[...], axis=0)[:1]
    inverse = lax.rsqrt(total / (channels * ntp) + EPSILON)
    inverse = jnp.transpose(jnp.broadcast_to(inverse, (rows, rows)))
    for at in range(0, channels, 128):
        at = slice(at, at + 128)
        out_ref[:, at] = (gbuf[:, at] * inverse * ng_ref[:, at]).astype(BF16)

    @pl.when(seq + 1 < nseq)
    def _():
        halo.wait_send()

    await_send(drecv, nx - 1, d_sem)
    await_send(tot_recv, GROUP - 1, t_sem)
    await_send(crecv, nx - 1, c_sem)
    for c in range(CHUNKS):
        await_send(srecv.at[c], nx - 1, s_sem.at[c])
        await_send(zrecv.at[c], GROUP - 1, zf_sem.at[c])

        @pl.when(group + 1 < ngroups)
        def _():
            remote(pout.at[c], pin.at[c], p_sem.at[c], next_group).wait_send()

        await_send(szbuf.at[c], GROUP - 1, zb_sem.at[c])
        await_send(yrecv.at[c], nx - 1, y_sem.at[c])
    await_send(ssrecv, ntp - 1, n_sem)


def per_device(
    x_in, bc_in, z_in, dt_raw, starts, conv_x, conv_bc, a_log, dt_bias, d_skip, norm_gain
):
    rows, channels = x_in.shape
    state = bc_in.shape[2]
    heads = dt_raw.shape[1]
    nx, ntp = NX, lax.axis_size("tp")
    nz = lax.axis_size("seq") // nx
    width = channels // nx // CHUNKS
    total_width = channels + 2 * state
    part = state // GROUP
    operands = (
        x_in,
        bc_in,
        z_in,
        dt_raw.T,
        starts.reshape(1, rows),
        conv_x,
        conv_bc,
        a_log.reshape(1, heads),
        dt_bias.reshape(1, heads),
        d_skip.reshape(1, heads),
        norm_gain.reshape(1, channels),
    )
    sems = pltpu.SemaphoreType.DMA
    return pl.pallas_call(
        functools.partial(kernel, nz, nx, ntp),
        out_shape=jax.ShapeDtypeStruct((rows, channels), BF16),
        in_specs=[pl.BlockSpec(memory_space=pltpu.HBM)] * len(operands),
        out_specs=pl.BlockSpec(memory_space=pltpu.VMEM),
        scratch_shapes=[
            *(pltpu.VMEM(operand.shape, operand.dtype) for operand in operands),
            pltpu.VMEM((4 * FOLD, total_width // FOLD), BF16),
            pltpu.VMEM((4 * FOLD, total_width // FOLD), BF16),
            pltpu.VMEM((HEAD, total_width), F32),
            pltpu.VMEM((REACH + 1, total_width), F32),
            pltpu.VMEM((rows, channels), BF16),
            pltpu.VMEM((rows, channels), BF16),
            pltpu.VMEM((rows, 2 * state), BF16),
            pltpu.VMEM((nx, rows, state), BF16),
            pltpu.VMEM((nx, CHUNKS, width), F32),
            pltpu.VMEM((nx, CHUNKS, width), F32),
            pltpu.VMEM((CHUNKS, width), F32),
            pltpu.VMEM((GROUP, CHUNKS, width), F32),
            pltpu.VMEM((CHUNKS, nx, state, width), BF16),
            pltpu.VMEM((CHUNKS, nx, state, width), BF16),
            pltpu.VMEM((CHUNKS, nx - 1, state, width), BF16),
            pltpu.VMEM((CHUNKS, nx - 1, rows, width), F32),
            pltpu.VMEM((CHUNKS, GROUP, part, width), BF16),
            pltpu.VMEM((CHUNKS, GROUP, part, width), BF16),
            pltpu.VMEM((CHUNKS, GROUP, part, width), F32),
            pltpu.VMEM((CHUNKS, part, width), BF16),
            pltpu.VMEM((CHUNKS, part, width), BF16),
            pltpu.VMEM((CHUNKS, GROUP, part, width), BF16),
            pltpu.VMEM((CHUNKS, GROUP, part, width), BF16),
            pltpu.VMEM((CHUNKS, nx, rows, width), BF16),
            pltpu.VMEM((CHUNKS, nx, rows, width), BF16),
            pltpu.VMEM((rows, channels), F32),
            pltpu.VMEM((rows, channels), F32),
            pltpu.VMEM((rows, channels), F32),
            pltpu.VMEM((rows, channels), F32),
            pltpu.VMEM((8, 128), F32),
            pltpu.VMEM((ntp, 8, 128), F32),
            sems((len(operands),)),
            sems((2,)),
            sems((2,)),
            sems((2,)),
            sems((2,)),
            sems((CHUNKS, 2)),
            sems((CHUNKS, 2)),
            sems((CHUNKS, 2)),
            sems((CHUNKS, 2)),
            sems((CHUNKS, 2)),
            sems((2,)),
            pltpu.SemaphoreType.REGULAR((2,)),
        ],
        compiler_params=pltpu.CompilerParams(
            collective_id=0, has_side_effects=True, vmem_limit_bytes=40 * 2**20
        ),
        cost_estimate=pl.CostEstimate(flops=2 * 10**8, bytes_accessed=2**20, transcendentals=10**6),
    )(*operands)


def solution(mesh):
    return jax.shard_map(
        per_device,
        mesh=mesh,
        in_specs=(
            P("seq", "tp"),
            P("seq", None, "tp"),
            P("seq", "tp"),
            P("seq", "tp"),
            P("seq"),
            P(None, "tp"),
            P(None, None, "tp"),
            P("tp"),
            P("tp"),
            P("tp"),
            P("tp"),
        ),
        out_specs=P("seq", "tp"),
        check_vma=False,
    )
```

```python
import functools

import jax
import jax.numpy as jnp
from jax import lax
from jax.experimental import pallas as pl
from jax.experimental.pallas import tpu as pltpu
from jax.sharding import PartitionSpec as P

NX = 4
GROUP = 4
CHUNKS = 2
HEAD = 16
REACH = 3
FOLD = 4
EPSILON = 1e-05
MESH = pl.DeviceIdType.MESH
F32, BF16 = jnp.float32, jnp.bfloat16


def dot(a, b):
    return jnp.dot(a, b, preferred_element_type=F32)


def dot_nt(a, b):
    return lax.dot_general(a, b, (((1,), (1,)), ((), ())), preferred_element_type=F32)


def dot_tn(a, b):
    return lax.dot_general(a, b, (((0,), (0,)), ((), ())), preferred_element_type=F32)


def iota(shape, axis):
    return lax.broadcasted_iota(jnp.int32, shape, axis)


def pieces(value, count):
    parts = []
    for _ in range(count):
        part = value.astype(BF16)
        parts.append(part)
        value = value - part.astype(F32)
    return jnp.concatenate(parts, axis=0)


def silu(value):
    return value * jax.nn.sigmoid(value)


def kernel(
    nz, nx, ntp,
    x_hbm, bc_hbm, z_hbm, dt_hbm, st_hbm, cx_hbm, cbc_hbm, al_hbm, db_hbm, ds_hbm, ng_hbm,
    out_ref,
    x_ref, bc_ref, z_ref, dt_ref, st_ref, cx_ref, cbc_ref, al_ref, db_ref, ds_ref, ng_ref,
    hsend, hrecv, pre, weights, xc, fx, bcv, crecv, dsend, drecv, tot_send, tot_recv,
    edge, erecv, sbuf, srecv, lbuf, ylbuf, tbuf, zrecv, prebuf, pout, pin, gsend, grecv, obuf, szbuf, ysend, yrecv,
    ebuf, yi, sz, gbuf, ssend, ssrecv,
    in_sem, h_sem, d_sem, t_sem, e_sem, c_sem, s_sem, zf_sem, p_sem, g_sem, zb_sem, y_sem, n_sem, near_sem,
):
    seq, tp = lax.axis_index("seq"), lax.axis_index("tp")
    mz, mx = seq // nx, seq % nx
    nseq, ngroups = nz * nx, nz // GROUP
    group, member = mz // GROUP, mz % GROUP
    rows, channels = x_ref.shape
    state = bc_ref.shape[2]
    heads = dt_ref.shape[0]
    quarter = channels // nx
    width = quarter // CHUNKS
    total_width = channels + 2 * state
    part = state // GROUP

    def seq_at(z, x):
        return {"seq": z * nx + x}

    def x_peer(r):
        q = (mx + r) % nx
        return q, seq_at(mz, q)

    def z_peer(r):
        k = (member + r) % GROUP
        return k, seq_at(group * GROUP + k, mx)

    def t_peer(r):
        return {"tp": (tp + r) % ntp}

    following, preceding = {"seq": seq + 1}, {"seq": seq - 1}
    next_group = seq_at(mz + GROUP, mx)

    def remote(src, dst, sem, device):
        return pltpu.make_async_remote_copy(
            src_ref=src, dst_ref=dst, send_sem=sem.at[0], recv_sem=sem.at[1],
            device_id=device, device_id_type=MESH,
        )

    def await_recv(buffer, count, sem):
        some = buffer.at[pl.ds(0, count)]
        remote(some, some, sem, x_peer(1)[1]).wait_recv()

    def await_send(buffer, count, sem):
        some = buffer.at[pl.ds(0, count)]
        remote(some, some, sem, x_peer(1)[1]).wait_send()

    loads = [
        pltpu.make_async_copy(src, dst, in_sem.at[k])
        for k, (src, dst) in enumerate([
            (st_hbm, st_ref), (dt_hbm, dt_ref), (al_hbm, al_ref), (db_hbm, db_ref),
            (x_hbm, x_ref), (bc_hbm, bc_ref), (cx_hbm, cx_ref), (cbc_hbm, cbc_ref),
            (z_hbm, z_ref), (ds_hbm, ds_ref), (ng_hbm, ng_ref),
        ])
    ]
    for load in loads:
        load.start()

    barrier = pltpu.get_barrier_semaphore()

    def greet(device, sem=barrier):
        pl.semaphore_signal(sem, inc=1, device_id=device, device_id_type=MESH)

    def greet_along_z(distance, sem):
        @pl.when(mz >= distance)
        def _():
            greet(seq_at(mz - distance, mx), sem)

        @pl.when(mz + distance < nz)
        def _():
            greet(seq_at(mz + distance, mx), sem)

    def both(distance):
        return (mz >= distance).astype(jnp.int32) + (mz + distance < nz).astype(jnp.int32)

    for r in range(1, nx):
        greet(x_peer(r)[1])
    for r in range(2, GROUP):
        @pl.when(member >= r)
        def _():
            greet(seq_at(mz - r, mx))

        @pl.when(member + r < GROUP)
        def _():
            greet(seq_at(mz + r, mx))

    greet_along_z(1, barrier)

    @pl.when(seq > 0)
    def _():
        greet(preceding)

    for r in range(1, ntp):
        greet(t_peer(r))
    greeted = (nx - 1) + (ntp - 1) + both(1) + (seq + 1 < nseq).astype(jnp.int32)
    for r in range(2, GROUP):
        greeted += (member >= r).astype(jnp.int32) + (member + r < GROUP).astype(jnp.int32)

    row, col = iota((rows, rows), 0), iota((rows, rows), 1)
    tril = (col <= row).astype(F32).astype(BF16)
    ranges = [tril, (col > row).astype(F32).astype(BF16)]
    for d in range(1, REACH + 1):
        ranges.append(((col <= row) & (col > row - d)).astype(F32).astype(BF16))
    spread = iota((heads, channels), 1) // (channels // heads) == iota((heads, channels), 0)
    spread = spread.astype(F32).astype(BF16)
    spread2 = jnp.concatenate([spread, spread], axis=0)
    for load in loads[:4]:
        load.wait()
    starts = jnp.broadcast_to(st_ref[...].astype(F32), (rows, rows)).astype(BF16)
    counts = dot_nt(jnp.concatenate(ranges, axis=0), starts)
    seg_col = counts[:rows]
    to_last = (counts[rows : 2 * rows] == 0.0).astype(F32)
    linked = (seg_col == dot_nt(starts, tril)) & (col <= row)
    from_first = (seg_col == 0.0).astype(F32)
    none_between = [counts[(d + 1) * rows : (d + 2) * rows] == 0.0 for d in range(1, REACH + 1)]
    taps = jnp.concatenate(
        [((col == row - d) & none_between[d - 1]).astype(F32).astype(BF16) for d in range(1, REACH + 1)],
        axis=0,
    )

    for load in loads[4:8]:
        load.wait()
    weights[:, :channels] = cx_ref[...]
    for k in range(REACH + 1):
        weights[k : k + 1, channels : channels + state] = cbc_ref[k, 0:1, :]
        weights[k : k + 1, channels + state :] = cbc_ref[k, 1:2, :]
    b_in, c_in = bc_ref[:, 0, :], bc_ref[:, 1, :]

    tail = slice(rows - 8, rows)
    last_rows = jnp.concatenate(
        [x_ref[tail, :].astype(F32), b_in[tail].astype(F32), c_in[tail].astype(F32)], axis=1
    )
    last_rows = (last_rows * to_last[tail, :1])[8 - FOLD :]
    piece = total_width // FOLD
    hsend[...] = jnp.concatenate(
        [last_rows[:, k * piece : (k + 1) * piece] for k in range(FOLD)], axis=0
    ).astype(BF16)

    def column(ref):
        square = (heads, heads)
        here = iota(square, 0) == iota(square, 1)
        return jnp.sum(jnp.where(here, jnp.broadcast_to(ref[...], square), 0.0), axis=1, keepdims=True)

    raw = dt_ref[...].astype(F32) + column(db_ref)
    step = jnp.maximum(raw, 0.0) + jnp.log1p(jnp.exp(-jnp.abs(raw)))
    decay = -jnp.exp(column(al_ref)) * step
    parts = dot_nt(pieces(decay, 3), tril)
    cumulative = parts[:heads] + parts[heads : 2 * heads] + parts[2 * heads :]
    ebuf[...] = dot_tn(pieces(jnp.exp(cumulative), 2), spread2)
    fall = ebuf[rows - 1 :, :]
    through = fall * (seg_col[rows - 1 : rows, :1] == 0.0).astype(F32)
    for q in range(nx):
        for c in range(CHUNKS):
            at = q * quarter + c * width
            dsend[q, c : c + 1, :] = through[:, at : at + width]
    factor = dot_tn(pieces(jnp.exp(-cumulative) * step, 2), spread2)

    def conv(values, at):
        size = values.shape[1]
        taken = weights[:, at : at + size]
        shifted = dot(taps, values)
        total = taken[REACH:] * values.astype(F32)
        for d in range(1, REACH + 1):
            total += taken[REACH - d : REACH - d + 1] * shifted[(d - 1) * rows : d * rows]
        pre[:, at : at + size] = total[:HEAD]
        return silu(total)

    bcv[:, :state] = conv(b_in, channels).astype(BF16)
    bcv[:, state:] = conv(c_in, channels + state).astype(BF16)
    for at in range(0, channels, 256):
        xc[:, at : at + 256] = conv(x_ref[:, at : at + 256], at).astype(BF16)

    for at in range(0, channels, 256):
        at = slice(at, at + 256)
        fx[:, at] = (xc[:, at].astype(F32) * factor[:, at]).astype(BF16)
    later = to_last * (row >= HEAD).astype(F32)
    bt = jnp.transpose(bcv[:, :state].astype(F32) * later[:, :1]).astype(BF16)
    for c in range(CHUNKS):
        for q in range(nx):
            at = slice(q * quarter + c * width, q * quarter + (c + 1) * width)
            sbuf[c, q] = (dot(bt, fx[:, at]) * fall[:, at]).astype(BF16)

    pl.semaphore_wait(barrier, greeted)

    halo = remote(hsend, hrecv, h_sem, following)

    @pl.when(seq + 1 < nseq)
    def _():
        halo.start()

    greet_along_z(1, near_sem.at[0])
    for r in range(1, nx):
        q, device = x_peer(r)
        remote(dsend.at[q], drecv.at[mx], d_sem, device).start()
    for c in range(CHUNKS):
        for r in range(1, nx):
            q, device = x_peer(r)
            remote(sbuf.at[c, q], srecv.at[c, mx], s_sem.at[c], device).start()
    drecv[mx] = dsend[mx]
    for c in range(CHUNKS):
        srecv[c, mx] = sbuf[c, mx]

    @pl.when(seq == 0)
    def _():
        hrecv[...] = jnp.zeros(hrecv.shape, BF16)

    @pl.when(seq > 0)
    def _():
        halo.wait_recv()

    place_row, place_col = iota((HEAD, HEAD), 0), iota((HEAD, HEAD), 1)
    for k in range(FOLD):
        at = slice(k * piece, (k + 1) * piece)
        reached = []
        for d in range(1, REACH + 1):
            here = (place_col - (k + 1) * FOLD == place_row - d) & (place_row < d)
            here &= none_between[d - 1][:HEAD, :HEAD] & (place_col >= k * FOLD)
            reached.append(here.astype(F32).astype(BF16))
        added = dot(jnp.concatenate(reached, axis=0), hrecv[...])
        total = pre[:, at]
        for d in range(1, REACH + 1):
            total += weights[REACH - d : REACH - d + 1, at] * added[(d - 1) * HEAD : d * HEAD]
        pre[:, at] = total
    done = silu(pre[...]).astype(BF16)
    xc[:HEAD, :] = done[:, :channels]
    bcv[:HEAD, :] = done[:, channels:]
    first_x = done[:, :channels].astype(F32) * factor[:HEAD]
    fx[:HEAD, :] = first_x.astype(BF16)
    first_x = (first_x * fall).astype(BF16)
    first_b = (done[:, channels : channels + state].astype(F32) * to_last[:HEAD, :1]).astype(BF16)
    for q in range(nx):
        edge[q, :, :state] = first_b
        edge[q, :, state:] = first_x[:, q * quarter : (q + 1) * quarter]
    erecv[mx] = edge[mx]
    for r in range(1, nx):
        q, device = x_peer(r)
        remote(edge.at[q], erecv.at[mx], e_sem, device).start()
    b, cc = bcv[:, :state], bcv[:, state:]
    crecv[mx] = cc
    for r in range(1, nx):
        _, device = x_peer(r)
        remote(crecv.at[mx], crecv.at[mx], c_sem, device).start()

    await_recv(drecv, nx - 1, d_sem)
    reach_of = [None, drecv[0]]
    for k in range(1, nx):
        reach_of.append(reach_of[-1] * drecv[k])
    tot_send[...] = reach_of[nx]
    tot_recv[member] = reach_of[nx]
    for r in range(1, GROUP):
        k, device = z_peer(r)
        remote(tot_send, tot_recv.at[member], t_sem, device).start()
    pl.semaphore_wait(near_sem.at[0], both(1))
    if GROUP > 2:
        greet_along_z(2, near_sem.at[1])

    scores = jnp.where(linked, dot_nt(cc, b), 0.0).astype(BF16)
    for q in range(nx):
        at = slice(q * quarter, (q + 1) * quarter)
        yi[:, at] = dot(scores, fx[:, at])
    for load in loads[8:]:
        load.wait()
    sz[...] = silu(z_ref[...].astype(F32))

    if GROUP > 2:
        pl.semaphore_wait(near_sem.at[1], both(2))
    if ngroups > 2:
        @pl.when(group == 2)
        def _():
            greet(seq_at(mz - GROUP, mx), near_sem.at[2])

    await_recv(erecv, nx - 1, e_sem)

    def made(c, k):
        first = dot_tn(erecv[k, :, :state], erecv[k, :, state + c * width : state + (c + 1) * width])
        return srecv[c, k].astype(F32) + first

    for c in range(CHUNKS):
        await_recv(srecv.at[c], nx - 1, s_sem.at[c])
        running = made(c, 0)
        for k in range(1, nx):
            lbuf[c, k - 1] = running.astype(BF16)
            running = drecv[k, c : c + 1, :] * running + made(c, k)
        tbuf[c] = running.astype(BF16).reshape(GROUP, part, width)
        zrecv[c, member] = tbuf[c, member]
        for r in range(1, GROUP):
            k, device = z_peer(r)
            remote(tbuf.at[c, k], zrecv.at[c, member], zf_sem.at[c], device).start()

    await_recv(crecv, nx - 1, c_sem)
    for c in range(CHUNKS):
        for k in range(1, nx):
            ylbuf[c, k - 1] = dot(crecv[k], lbuf[c, k - 1])

    await_recv(tot_recv, GROUP - 1, t_sem)
    row_fall = [tot_recv[k] for k in range(GROUP)]
    group_fall = row_fall[0]
    for k in range(1, GROUP):
        group_fall = row_fall[k] * group_fall
    even = group % 2 == 0
    share_decay = remote(gsend, grecv, g_sem, next_group)

    def hand_on(c, slot, device, sent=0):
        return pltpu.make_async_remote_copy(
            src_ref=pout.at[c], dst_ref=pin.at[c, slot],
            send_sem=p_sem.at[c, sent], recv_sem=p_sem.at[c, 2 + slot],
            device_id=device, device_id_type=MESH,
        )

    after_next_group = seq_at(mz + 2 * GROUP, mx)

    @pl.when(even)
    def _():
        gsend[...] = group_fall
        share_decay.start()
        grecv[...] = jnp.ones(grecv.shape, F32)
        pin[:, 0] = jnp.zeros((CHUNKS, part, width), BF16)

    @pl.when(group < 2)
    def _():
        pin[:, 1] = jnp.zeros((CHUNKS, part, width), BF16)

    group_totals = []
    for c in range(CHUNKS):
        await_recv(zrecv.at[c], GROUP - 1, zf_sem.at[c])
        running = zrecv[c, 0].astype(F32)
        for k in range(1, GROUP):
            prebuf[c, k] = running
            running = row_fall[k][c : c + 1] * running + zrecv[c, k].astype(F32)
        group_totals.append(running)

        @pl.when(even)
        def _():
            pout[c] = running.astype(BF16)
            hand_on(c, 0, next_group).start()

    @pl.when(jnp.logical_not(even))
    def _():
        share_decay.wait_recv()
        for c in range(CHUNKS):
            hand_on(c, 0, next_group).wait_recv()

    if ngroups > 2:
        @pl.when(group == 1)
        def _():
            pl.semaphore_wait(near_sem.at[2], 1)
            for c in range(CHUNKS):
                reached = group_fall[c : c + 1] * pin[c, 0].astype(F32) + group_totals[c]
                pout[c] = reached.astype(BF16)
                hand_on(c, 1, after_next_group, 1).start()
                hand_on(c, 1, next_group).start()

    for c in range(CHUNKS):
        if ngroups > 2:
            @pl.when(group >= 2)
            def _():
                hand_on(c, 1, next_group).wait_recv()

        before = grecv[c : c + 1] * pin[c, 1].astype(F32) + pin[c, 0].astype(F32)
        obuf[c, 0] = before.astype(BF16)
        reach = row_fall[0][c : c + 1]
        for k in range(1, GROUP):
            obuf[c, k] = (reach * before + prebuf[c, k]).astype(BF16)
            reach = row_fall[k][c : c + 1] * reach
        szbuf[c, member] = obuf[c, member]
        for r in range(1, GROUP):
            k, device = z_peer(r)
            remote(obuf.at[c, k], szbuf.at[c, member], zb_sem.at[c], device).start()

    for c in range(CHUNKS):
        await_recv(szbuf.at[c], GROUP - 1, zb_sem.at[c])
        entering = szbuf[c].reshape(state, width)
        for k in range(nx):
            part_y = dot(crecv[k], entering)
            if k:
                part_y = reach_of[k][c : c + 1, :] * part_y + ylbuf[c, k - 1]
            ysend[c, k] = part_y.astype(BF16)
        yrecv[c, mx] = ysend[c, mx]
        for r in range(1, nx):
            q, device = x_peer(r)
            remote(ysend.at[c, q], yrecv.at[c, mx], y_sem.at[c], device).start()

    skip = dot_tn(pieces(jnp.broadcast_to(column(ds_ref), (heads, 128)), 2), spread2)[:1]
    squares = jnp.zeros((rows, 128), F32)
    for c in range(CHUNKS):
        await_recv(yrecv.at[c], nx - 1, y_sem.at[c])
        for q in range(nx):
            at = slice(q * quarter + c * width, q * quarter + (c + 1) * width)
            y = yi[:, at] + from_first[:, :1] * yrecv[c, q].astype(F32)
            y = ebuf[:, at] * y + skip[:, at] * xc[:, at].astype(F32)
            gated = y * sz[:, at]
            gbuf[:, at] = gated
            for k in range(0, width, 128):
                some = gated[:, k : k + 128]
                squares += some * some
    total = jnp.sum(jnp.transpose(squares), axis=0, keepdims=True)
    total = jnp.broadcast_to(total, ssend.shape)
    ssend[...] = total
    ssrecv[tp] = total
    for r in range(1, ntp):
        remote(ssend, ssrecv.at[tp], n_sem, t_peer(r)).start()
    await_recv(ssrecv, ntp - 1, n_sem)
    total = jnp.sum(ssrecv[...], axis=0)[:1]
    inverse = lax.rsqrt(total / (channels * ntp) + EPSILON)
    inverse = jnp.transpose(jnp.broadcast_to(inverse, (rows, rows)))
    for at in range(0, channels, 128):
        at = slice(at, at + 128)
        out_ref[:, at] = (gbuf[:, at] * inverse * ng_ref[:, at]).astype(BF16)

    @pl.when(seq + 1 < nseq)
    def _():
        halo.wait_send()

    await_send(drecv, nx - 1, d_sem)
    await_send(tot_recv, GROUP - 1, t_sem)
    await_send(erecv, nx - 1, e_sem)
    await_send(crecv, nx - 1, c_sem)
    for c in range(CHUNKS):
        await_send(srecv.at[c], nx - 1, s_sem.at[c])
        await_send(zrecv.at[c], GROUP - 1, zf_sem.at[c])

        @pl.when(even)
        def _():
            if c == 0:
                share_decay.wait_send()
            hand_on(c, 0, next_group).wait_send()

        if ngroups > 2:
            @pl.when(group == 1)
            def _():
                hand_on(c, 1, next_group).wait_send()
                hand_on(c, 1, after_next_group, 1).wait_send()

        await_send(szbuf.at[c], GROUP - 1, zb_sem.at[c])
        await_send(yrecv.at[c], nx - 1, y_sem.at[c])
    await_send(ssrecv, ntp - 1, n_sem)


def per_device(
    x_in, bc_in, z_in, dt_raw, starts, conv_x, conv_bc, a_log, dt_bias, d_skip, norm_gain
):
    rows, channels = x_in.shape
    state = bc_in.shape[2]
    heads = dt_raw.shape[1]
    nx, ntp = NX, lax.axis_size("tp")
    nz = lax.axis_size("seq") // nx
    width = channels // nx // CHUNKS
    total_width = channels + 2 * state
    part = state // GROUP
    operands = (
        x_in,
        bc_in,
        z_in,
        dt_raw.T,
        starts.reshape(1, rows),
        conv_x,
        conv_bc,
        a_log.reshape(1, heads),
        dt_bias.reshape(1, heads),
        d_skip.reshape(1, heads),
        norm_gain.reshape(1, channels),
    )
    operands = tuple(pltpu.with_memory_space_constraint(o, pltpu.HBM) for o in operands)
    sems = pltpu.SemaphoreType.DMA
    return pl.pallas_call(
        functools.partial(kernel, nz, nx, ntp),
        out_shape=jax.ShapeDtypeStruct((rows, channels), BF16),
        in_specs=[pl.BlockSpec(memory_space=pltpu.HBM)] * len(operands),
        out_specs=pl.BlockSpec(memory_space=pltpu.VMEM),
        scratch_shapes=[
            *(pltpu.VMEM(operand.shape, operand.dtype) for operand in operands),
            pltpu.VMEM((4 * FOLD, total_width // FOLD), BF16),
            pltpu.VMEM((4 * FOLD, total_width // FOLD), BF16),
            pltpu.VMEM((HEAD, total_width), F32),
            pltpu.VMEM((REACH + 1, total_width), F32),
            pltpu.VMEM((rows, channels), BF16),
            pltpu.VMEM((rows, channels), BF16),
            pltpu.VMEM((rows, 2 * state), BF16),
            pltpu.VMEM((nx, rows, state), BF16),
            pltpu.VMEM((nx, CHUNKS, width), F32),
            pltpu.VMEM((nx, CHUNKS, width), F32),
            pltpu.VMEM((CHUNKS, width), F32),
            pltpu.VMEM((GROUP, CHUNKS, width), F32),
            pltpu.VMEM((nx, HEAD, state + width * CHUNKS), BF16),
            pltpu.VMEM((nx, HEAD, state + width * CHUNKS), BF16),
            pltpu.VMEM((CHUNKS, nx, state, width), BF16),
            pltpu.VMEM((CHUNKS, nx, state, width), BF16),
            pltpu.VMEM((CHUNKS, nx - 1, state, width), BF16),
            pltpu.VMEM((CHUNKS, nx - 1, rows, width), F32),
            pltpu.VMEM((CHUNKS, GROUP, part, width), BF16),
            pltpu.VMEM((CHUNKS, GROUP, part, width), BF16),
            pltpu.VMEM((CHUNKS, GROUP, part, width), F32),
            pltpu.VMEM((CHUNKS, part, width), BF16),
            pltpu.VMEM((CHUNKS, 2, part, width), BF16),
            pltpu.VMEM((CHUNKS, width), F32),
            pltpu.VMEM((CHUNKS, width), F32),
            pltpu.VMEM((CHUNKS, GROUP, part, width), BF16),
            pltpu.VMEM((CHUNKS, GROUP, part, width), BF16),
            pltpu.VMEM((CHUNKS, nx, rows, width), BF16),
            pltpu.VMEM((CHUNKS, nx, rows, width), BF16),
            pltpu.VMEM((rows, channels), F32),
            pltpu.VMEM((rows, channels), F32),
            pltpu.VMEM((rows, channels), F32),
            pltpu.VMEM((rows, channels), F32),
            pltpu.VMEM((1, 128), F32),
            pltpu.VMEM((ntp, 1, 128), F32),
            sems((len(operands),)),
            sems((2,)),
            sems((2,)),
            sems((2,)),
            sems((2,)),
            sems((2,)),
            sems((CHUNKS, 2)),
            sems((CHUNKS, 2)),
            sems((CHUNKS, 4)),
            sems((2,)),
            sems((CHUNKS, 2)),
            sems((CHUNKS, 2)),
            sems((2,)),
            pltpu.SemaphoreType.REGULAR((3,)),
        ],
        compiler_params=pltpu.CompilerParams(
            collective_id=0, has_side_effects=True, vmem_limit_bytes=40 * 2**20
        ),
        cost_estimate=pl.CostEstimate(flops=2 * 10**8, bytes_accessed=2**20, transcendentals=10**6),
    )(*operands)


def solution(mesh):
    return jax.shard_map(
        per_device,
        mesh=mesh,
        in_specs=(
            P("seq", "tp"),
            P("seq", None, "tp"),
            P("seq", "tp"),
            P("seq", "tp"),
            P("seq"),
            P(None, "tp"),
            P(None, None, "tp"),
            P("tp"),
            P("tp"),
            P("tp"),
            P("tp"),
        ),
        out_specs=P("seq", "tp"),
        check_vma=False,
    )
```

```python
import functools

import jax
import jax.numpy as jnp
from jax import lax
from jax.experimental import pallas as pl
from jax.experimental.pallas import tpu as pltpu
from jax.sharding import PartitionSpec as P

NX = 4
GROUP = 4
CHUNKS = 2
HEAD = 16
REACH = 3
FOLD = 4
EPSILON = 1e-05
MESH = pl.DeviceIdType.MESH
F32, BF16 = jnp.float32, jnp.bfloat16


def dot(a, b):
    return jnp.dot(a, b, preferred_element_type=F32)


def dot_nt(a, b):
    return lax.dot_general(a, b, (((1,), (1,)), ((), ())), preferred_element_type=F32)


def dot_tn(a, b):
    return lax.dot_general(a, b, (((0,), (0,)), ((), ())), preferred_element_type=F32)


def iota(shape, axis):
    return lax.broadcasted_iota(jnp.int32, shape, axis)


def pieces(value, count):
    parts = []
    for _ in range(count):
        part = value.astype(BF16)
        parts.append(part)
        value = value - part.astype(F32)
    return jnp.concatenate(parts, axis=0)


def silu(value):
    return value * jax.nn.sigmoid(value)


def kernel(
    nz, nx, ntp,
    x_hbm, bc_hbm, z_hbm, dt_hbm, st_hbm, cx_hbm, cbc_hbm, al_hbm, db_hbm, ds_hbm, ng_hbm,
    out_ref,
    x_ref, bc_ref, z_ref, dt_ref, st_ref, cx_ref, cbc_ref, al_ref, db_ref, ds_ref, ng_ref,
    hsend, hrecv, pre, weights, xc, fx, bcv, crecv, dsend, drecv, tot_send, tot_recv,
    edge, erecv, sbuf, srecv, lbuf, ylbuf, tbuf, zrecv, prebuf, pout, pin, gsend, grecv, obuf, szbuf, ysend, yrecv,
    ebuf, yi, sz, gbuf, ssend, ssrecv,
    in_sem, h_sem, d_sem, t_sem, e_sem, c_sem, s_sem, zf_sem, p_sem, g_sem, zb_sem, y_sem, n_sem, near_sem,
):
    seq, tp = lax.axis_index("seq"), lax.axis_index("tp")
    mz, mx = seq // nx, seq % nx
    nseq, ngroups = nz * nx, nz // GROUP
    group, member = mz // GROUP, mz % GROUP
    rows, channels = x_ref.shape
    state = bc_ref.shape[2]
    heads = dt_ref.shape[0]
    quarter = channels // nx
    width = quarter // CHUNKS
    total_width = channels + 2 * state
    part = state // GROUP

    def seq_at(z, x):
        return {"seq": z * nx + x}

    def x_peer(r):
        q = (mx + r) % nx
        return q, seq_at(mz, q)

    def z_peer(r):
        k = (member + r) % GROUP
        return k, seq_at(group * GROUP + k, mx)

    def t_peer(r):
        return {"tp": (tp + r) % ntp}

    following, preceding = {"seq": seq + 1}, {"seq": seq - 1}
    next_group = seq_at(mz + GROUP, mx)

    def remote(src, dst, sem, device):
        return pltpu.make_async_remote_copy(
            src_ref=src, dst_ref=dst, send_sem=sem.at[0], recv_sem=sem.at[1],
            device_id=device, device_id_type=MESH,
        )

    def await_recv(buffer, count, sem):
        some = buffer.at[pl.ds(0, count)]
        remote(some, some, sem, x_peer(1)[1]).wait_recv()

    def await_send(buffer, count, sem):
        some = buffer.at[pl.ds(0, count)]
        remote(some, some, sem, x_peer(1)[1]).wait_send()

    loads = [
        pltpu.make_async_copy(src, dst, in_sem.at[k])
        for k, (src, dst) in enumerate([
            (st_hbm, st_ref), (dt_hbm, dt_ref), (al_hbm, al_ref), (db_hbm, db_ref),
            (x_hbm, x_ref), (bc_hbm, bc_ref), (cx_hbm, cx_ref), (cbc_hbm, cbc_ref),
            (z_hbm, z_ref), (ds_hbm, ds_ref), (ng_hbm, ng_ref),
        ])
    ]
    for load in loads:
        load.start()

    barrier = pltpu.get_barrier_semaphore()

    def greet(device, sem=barrier):
        pl.semaphore_signal(sem, inc=1, device_id=device, device_id_type=MESH)

    def greet_along_z(distance, sem):
        @pl.when(mz >= distance)
        def _():
            greet(seq_at(mz - distance, mx), sem)

        @pl.when(mz + distance < nz)
        def _():
            greet(seq_at(mz + distance, mx), sem)

    def both(distance):
        return (mz >= distance).astype(jnp.int32) + (mz + distance < nz).astype(jnp.int32)

    for r in range(1, nx):
        greet(x_peer(r)[1])
    for r in range(2, GROUP):
        @pl.when(member >= r)
        def _():
            greet(seq_at(mz - r, mx))

        @pl.when(member + r < GROUP)
        def _():
            greet(seq_at(mz + r, mx))

    greet_along_z(1, barrier)

    @pl.when(seq > 0)
    def _():
        greet(preceding)

    for r in range(1, ntp):
        greet(t_peer(r))
    greeted = (nx - 1) + (ntp - 1) + both(1) + (seq + 1 < nseq).astype(jnp.int32)
    for r in range(2, GROUP):
        greeted += (member >= r).astype(jnp.int32) + (member + r < GROUP).astype(jnp.int32)

    row, col = iota((rows, rows), 0), iota((rows, rows), 1)
    tril = (col <= row).astype(F32).astype(BF16)
    ranges = [tril, (col > row).astype(F32).astype(BF16)]
    for d in range(1, REACH + 1):
        ranges.append(((col <= row) & (col > row - d)).astype(F32).astype(BF16))
    spread = iota((heads, channels), 1) // (channels // heads) == iota((heads, channels), 0)
    spread = spread.astype(F32).astype(BF16)
    spread2 = jnp.concatenate([spread, spread], axis=0)
    for load in loads[:4]:
        load.wait()
    starts = jnp.broadcast_to(st_ref[...].astype(F32), (rows, rows)).astype(BF16)
    counts = dot_nt(jnp.concatenate(ranges, axis=0), starts)
    seg_col = counts[:rows]
    to_last = (counts[rows : 2 * rows] == 0.0).astype(F32)
    linked = (seg_col == dot_nt(starts, tril)) & (col <= row)
    from_first = (seg_col == 0.0).astype(F32)
    none_between = [counts[(d + 1) * rows : (d + 2) * rows] == 0.0 for d in range(1, REACH + 1)]
    taps = jnp.concatenate(
        [((col == row - d) & none_between[d - 1]).astype(F32).astype(BF16) for d in range(1, REACH + 1)],
        axis=0,
    )

    for load in loads[4:8]:
        load.wait()
    weights[:, :channels] = cx_ref[...]
    for k in range(REACH + 1):
        weights[k : k + 1, channels : channels + state] = cbc_ref[k, 0:1, :]
        weights[k : k + 1, channels + state :] = cbc_ref[k, 1:2, :]
    b_in, c_in = bc_ref[:, 0, :], bc_ref[:, 1, :]

    tail = slice(rows - 8, rows)
    last_rows = jnp.concatenate(
        [x_ref[tail, :].astype(F32), b_in[tail].astype(F32), c_in[tail].astype(F32)], axis=1
    )
    last_rows = (last_rows * to_last[tail, :1])[8 - FOLD :]
    piece = total_width // FOLD
    hsend[...] = jnp.concatenate(
        [last_rows[:, k * piece : (k + 1) * piece] for k in range(FOLD)], axis=0
    ).astype(BF16)

    def column(ref):
        square = (heads, heads)
        here = iota(square, 0) == iota(square, 1)
        return jnp.sum(jnp.where(here, jnp.broadcast_to(ref[...], square), 0.0), axis=1, keepdims=True)

    raw = dt_ref[...].astype(F32) + column(db_ref)
    step = jnp.maximum(raw, 0.0) + jnp.log1p(jnp.exp(-jnp.abs(raw)))
    decay = -jnp.exp(column(al_ref)) * step
    parts = dot_nt(pieces(decay, 3), tril)
    cumulative = parts[:heads] + parts[heads : 2 * heads] + parts[2 * heads :]
    ebuf[...] = dot_tn(pieces(jnp.exp(cumulative), 2), spread2)
    fall = ebuf[rows - 1 :, :]
    through = fall * (seg_col[rows - 1 : rows, :1] == 0.0).astype(F32)
    for q in range(nx):
        for c in range(CHUNKS):
            at = q * quarter + c * width
            dsend[q, c : c + 1, :] = through[:, at : at + width]
    factor = dot_tn(pieces(jnp.exp(-cumulative) * step, 2), spread2)

    def conv(values, at):
        size = values.shape[1]
        taken = weights[:, at : at + size]
        shifted = dot(taps, values)
        total = taken[REACH:] * values.astype(F32)
        for d in range(1, REACH + 1):
            total += taken[REACH - d : REACH - d + 1] * shifted[(d - 1) * rows : d * rows]
        pre[:, at : at + size] = total[:HEAD]
        return silu(total)

    bcv[:, :state] = conv(b_in, channels).astype(BF16)
    bcv[:, state:] = conv(c_in, channels + state).astype(BF16)
    for at in range(0, channels, 256):
        xc[:, at : at + 256] = conv(x_ref[:, at : at + 256], at).astype(BF16)

    for at in range(0, channels, 256):
        at = slice(at, at + 256)
        fx[:, at] = (xc[:, at].astype(F32) * factor[:, at]).astype(BF16)
    later = to_last * (row >= HEAD).astype(F32)
    bt = jnp.transpose(bcv[:, :state].astype(F32) * later[:, :1]).astype(BF16)
    for c in range(CHUNKS):
        for q in range(nx):
            at = slice(q * quarter + c * width, q * quarter + (c + 1) * width)
            sbuf[c, q] = (dot(bt, fx[:, at]) * fall[:, at]).astype(BF16)

    place_row, place_col = iota((HEAD, HEAD), 0), iota((HEAD, HEAD), 1)
    reached = []
    for k in range(FOLD):
        matrices = []
        for d in range(1, REACH + 1):
            here = (place_col - (k + 1) * FOLD == place_row - d) & (place_row < d)
            here &= none_between[d - 1][:HEAD, :HEAD] & (place_col >= k * FOLD)
            matrices.append(here.astype(F32).astype(BF16))
        reached.append(jnp.concatenate(matrices, axis=0))

    pl.semaphore_wait(barrier, greeted)

    halo = remote(hsend, hrecv, h_sem, following)

    @pl.when(seq + 1 < nseq)
    def _():
        halo.start()

    greet_along_z(1, near_sem.at[0])
    for r in range(1, nx):
        q, device = x_peer(r)
        remote(dsend.at[q], drecv.at[mx], d_sem, device).start()
    def send_states(c):
        for r in (2, 1, 3) if nx == 4 else range(1, nx):
            q, device = x_peer(r)
            remote(sbuf.at[c, q], srecv.at[c, mx], s_sem.at[c], device).start()

    send_states(0)
    drecv[mx] = dsend[mx]
    for c in range(CHUNKS):
        srecv[c, mx] = sbuf[c, mx]

    @pl.when(seq == 0)
    def _():
        hrecv[...] = jnp.zeros(hrecv.shape, BF16)

    @pl.when(seq > 0)
    def _():
        halo.wait_recv()

    for k in range(FOLD):
        at = slice(k * piece, (k + 1) * piece)
        added = dot(reached[k], hrecv[...])
        total = pre[:, at]
        for d in range(1, REACH + 1):
            total += weights[REACH - d : REACH - d + 1, at] * added[(d - 1) * HEAD : d * HEAD]
        pre[:, at] = total
    done = silu(pre[...]).astype(BF16)
    xc[:HEAD, :] = done[:, :channels]
    bcv[:HEAD, :] = done[:, channels:]
    first_x = done[:, :channels].astype(F32) * factor[:HEAD]
    fx[:HEAD, :] = first_x.astype(BF16)
    first_x = (first_x * fall).astype(BF16)
    first_b = (done[:, channels : channels + state].astype(F32) * to_last[:HEAD, :1]).astype(BF16)
    for q in range(nx):
        edge[q, :, :state] = first_b
        edge[q, :, state:] = first_x[:, q * quarter : (q + 1) * quarter]
    erecv[mx] = edge[mx]
    for r in range(1, nx):
        q, device = x_peer(r)
        remote(edge.at[q], erecv.at[mx], e_sem, device).start()
    for c in range(1, CHUNKS):
        send_states(c)
    b, cc = bcv[:, :state], bcv[:, state:]
    crecv[mx] = cc

    await_recv(drecv, nx - 1, d_sem)
    reach_of = [None, drecv[0]]
    for k in range(1, nx):
        reach_of.append(reach_of[-1] * drecv[k])
    tot_send[...] = reach_of[nx]
    tot_recv[member] = reach_of[nx]
    for r in range(1, GROUP):
        k, device = z_peer(r)
        remote(tot_send, tot_recv.at[member], t_sem, device).start()
    pl.semaphore_wait(near_sem.at[0], both(1))
    if GROUP > 2:
        greet_along_z(2, near_sem.at[1])

    scores = jnp.where(linked, dot_nt(cc, b), 0.0).astype(BF16)
    for load in loads[8:]:
        load.wait()
    skip = dot_tn(pieces(jnp.broadcast_to(column(ds_ref), (heads, 128)), 2), spread2)[:1]
    for q in range(nx):
        at = slice(q * quarter, (q + 1) * quarter)
        gate = silu(z_ref[:, at].astype(F32))
        own = ebuf[:, at] * dot(scores, fx[:, at]) + skip[:, at] * xc[:, at].astype(F32)
        yi[:, at] = own * gate
        sz[:, at] = ebuf[:, at] * from_first[:, :1] * gate

    if GROUP > 2:
        pl.semaphore_wait(near_sem.at[1], both(2))
    if ngroups > 2:
        @pl.when(group == 2)
        def _():
            greet(seq_at(mz - GROUP, mx), near_sem.at[2])

    await_recv(erecv, nx - 1, e_sem)

    def made(c, k):
        first = dot_tn(erecv[k, :, :state], erecv[k, :, state + c * width : state + (c + 1) * width])
        return srecv[c, k].astype(F32) + first

    for c in range(CHUNKS):
        await_recv(srecv.at[c], nx - 1, s_sem.at[c])
        running = made(c, 0)
        for k in range(1, nx):
            lbuf[c, k - 1] = running.astype(BF16)
            running = drecv[k, c : c + 1, :] * running + made(c, k)
        tbuf[c] = running.astype(BF16).reshape(GROUP, part, width)
        zrecv[c, member] = tbuf[c, member]
        for r in range(1, GROUP):
            k, device = z_peer(r)
            remote(tbuf.at[c, k], zrecv.at[c, member], zf_sem.at[c], device).start()

    for r in range(1, nx):
        _, device = x_peer(r)
        remote(crecv.at[mx], crecv.at[mx], c_sem, device).start()

    await_recv(tot_recv, GROUP - 1, t_sem)
    row_fall = [tot_recv[k] for k in range(GROUP)]
    group_fall = row_fall[0]
    for k in range(1, GROUP):
        group_fall = row_fall[k] * group_fall
    even = group % 2 == 0
    share_decay = remote(gsend, grecv, g_sem, next_group)

    def hand_on(c, slot, device, sent=0):
        return pltpu.make_async_remote_copy(
            src_ref=pout.at[c], dst_ref=pin.at[c, slot],
            send_sem=p_sem.at[c, sent], recv_sem=p_sem.at[c, 2 + slot],
            device_id=device, device_id_type=MESH,
        )

    after_next_group = seq_at(mz + 2 * GROUP, mx)

    @pl.when(even)
    def _():
        gsend[...] = group_fall
        share_decay.start()
        grecv[...] = jnp.ones(grecv.shape, F32)
        pin[:, 0] = jnp.zeros((CHUNKS, part, width), BF16)

    @pl.when(group < 2)
    def _():
        pin[:, 1] = jnp.zeros((CHUNKS, part, width), BF16)

    group_totals = []
    for c in range(CHUNKS):
        await_recv(zrecv.at[c], GROUP - 1, zf_sem.at[c])
        running = zrecv[c, 0].astype(F32)
        for k in range(1, GROUP):
            prebuf[c, k] = running
            running = row_fall[k][c : c + 1] * running + zrecv[c, k].astype(F32)
        group_totals.append(running)

        @pl.when(even)
        def _():
            pout[c] = running.astype(BF16)
            hand_on(c, 0, next_group).start()

    @pl.when(jnp.logical_not(even))
    def _():
        share_decay.wait_recv()
        for c in range(CHUNKS):
            hand_on(c, 0, next_group).wait_recv()

    if ngroups > 2:
        @pl.when(group == 1)
        def _():
            pl.semaphore_wait(near_sem.at[2], 1)
            for c in range(CHUNKS):
                reached = group_fall[c : c + 1] * pin[c, 0].astype(F32) + group_totals[c]
                pout[c] = reached.astype(BF16)
                hand_on(c, 1, after_next_group, 1).start()
                hand_on(c, 1, next_group).start()

    for c in range(CHUNKS):
        if ngroups > 2:
            @pl.when(group >= 2)
            def _():
                hand_on(c, 1, next_group).wait_recv()

        before = grecv[c : c + 1] * pin[c, 1].astype(F32) + pin[c, 0].astype(F32)
        obuf[c, 0] = before.astype(BF16)
        reach = row_fall[0][c : c + 1]
        for k in range(1, GROUP):
            obuf[c, k] = (reach * before + prebuf[c, k]).astype(BF16)
            reach = row_fall[k][c : c + 1] * reach
        szbuf[c, member] = obuf[c, member]
        for r in range(1, GROUP):
            k, device = z_peer(r)
            remote(obuf.at[c, k], szbuf.at[c, member], zb_sem.at[c], device).start()

    await_recv(crecv, nx - 1, c_sem)
    for c in range(CHUNKS):
        for k in range(1, nx):
            ylbuf[c, k - 1] = dot(crecv[k], lbuf[c, k - 1])

    for c in range(CHUNKS):
        await_recv(szbuf.at[c], GROUP - 1, zb_sem.at[c])
        entering = szbuf[c].reshape(state, width)
        for k in range(nx):
            part_y = dot(crecv[k], entering)
            if k:
                part_y = reach_of[k][c : c + 1, :] * part_y + ylbuf[c, k - 1]
            ysend[c, k] = part_y.astype(BF16)
        yrecv[c, mx] = ysend[c, mx]
        for r in range(1, nx):
            q, device = x_peer(r)
            remote(ysend.at[c, q], yrecv.at[c, mx], y_sem.at[c], device).start()

    squares = jnp.zeros((rows, 128), F32)
    for c in range(CHUNKS):
        await_recv(yrecv.at[c], nx - 1, y_sem.at[c])
        for q in range(nx):
            at = slice(q * quarter + c * width, q * quarter + (c + 1) * width)
            gated = yi[:, at] + sz[:, at] * yrecv[c, q].astype(F32)
            gbuf[:, at] = gated
            for k in range(0, width, 128):
                some = gated[:, k : k + 128]
                squares += some * some
    total = jnp.sum(jnp.transpose(squares), axis=0, keepdims=True)
    total = jnp.broadcast_to(total, ssend.shape)
    ssend[...] = total
    ssrecv[tp] = total
    for r in range(1, ntp):
        remote(ssend, ssrecv.at[tp], n_sem, t_peer(r)).start()
    await_recv(ssrecv, ntp - 1, n_sem)
    total = jnp.sum(ssrecv[...], axis=0)[:1]
    inverse = lax.rsqrt(total / (channels * ntp) + EPSILON)
    inverse = jnp.transpose(jnp.broadcast_to(inverse, (rows, rows)))
    for at in range(0, channels, 128):
        at = slice(at, at + 128)
        out_ref[:, at] = (gbuf[:, at] * inverse * ng_ref[:, at]).astype(BF16)

    @pl.when(seq + 1 < nseq)
    def _():
        halo.wait_send()

    await_send(drecv, nx - 1, d_sem)
    await_send(tot_recv, GROUP - 1, t_sem)
    await_send(erecv, nx - 1, e_sem)
    await_send(crecv, nx - 1, c_sem)
    for c in range(CHUNKS):
        await_send(srecv.at[c], nx - 1, s_sem.at[c])
        await_send(zrecv.at[c], GROUP - 1, zf_sem.at[c])

        @pl.when(even)
        def _():
            if c == 0:
                share_decay.wait_send()
            hand_on(c, 0, next_group).wait_send()

        if ngroups > 2:
            @pl.when(group == 1)
            def _():
                hand_on(c, 1, next_group).wait_send()
                hand_on(c, 1, after_next_group, 1).wait_send()

        await_send(szbuf.at[c], GROUP - 1, zb_sem.at[c])
        await_send(yrecv.at[c], nx - 1, y_sem.at[c])
    await_send(ssrecv, ntp - 1, n_sem)


def per_device(
    x_in, bc_in, z_in, dt_raw, starts, conv_x, conv_bc, a_log, dt_bias, d_skip, norm_gain
):
    rows, channels = x_in.shape
    state = bc_in.shape[2]
    heads = dt_raw.shape[1]
    nx, ntp = NX, lax.axis_size("tp")
    nz = lax.axis_size("seq") // nx
    width = channels // nx // CHUNKS
    total_width = channels + 2 * state
    part = state // GROUP
    operands = (
        x_in,
        bc_in,
        z_in,
        dt_raw.T,
        starts.reshape(1, rows),
        conv_x,
        conv_bc,
        a_log.reshape(1, heads),
        dt_bias.reshape(1, heads),
        d_skip.reshape(1, heads),
        norm_gain.reshape(1, channels),
    )
    operands = tuple(pltpu.with_memory_space_constraint(o, pltpu.HBM) for o in operands)
    sems = pltpu.SemaphoreType.DMA
    return pl.pallas_call(
        functools.partial(kernel, nz, nx, ntp),
        out_shape=jax.ShapeDtypeStruct((rows, channels), BF16),
        in_specs=[pl.BlockSpec(memory_space=pltpu.HBM)] * len(operands),
        out_specs=pl.BlockSpec(memory_space=pltpu.VMEM),
        scratch_shapes=[
            *(pltpu.VMEM(operand.shape, operand.dtype) for operand in operands),
            pltpu.VMEM((4 * FOLD, total_width // FOLD), BF16),
            pltpu.VMEM((4 * FOLD, total_width // FOLD), BF16),
            pltpu.VMEM((HEAD, total_width), F32),
            pltpu.VMEM((REACH + 1, total_width), F32),
            pltpu.VMEM((rows, channels), BF16),
            pltpu.VMEM((rows, channels), BF16),
            pltpu.VMEM((rows, 2 * state), BF16),
            pltpu.VMEM((nx, rows, state), BF16),
            pltpu.VMEM((nx, CHUNKS, width), F32),
            pltpu.VMEM((nx, CHUNKS, width), F32),
            pltpu.VMEM((CHUNKS, width), F32),
            pltpu.VMEM((GROUP, CHUNKS, width), F32),
            pltpu.VMEM((nx, HEAD, state + width * CHUNKS), BF16),
            pltpu.VMEM((nx, HEAD, state + width * CHUNKS), BF16),
            pltpu.VMEM((CHUNKS, nx, state, width), BF16),
            pltpu.VMEM((CHUNKS, nx, state, width), BF16),
            pltpu.VMEM((CHUNKS, nx - 1, state, width), BF16),
            pltpu.VMEM((CHUNKS, nx - 1, rows, width), F32),
            pltpu.VMEM((CHUNKS, GROUP, part, width), BF16),
            pltpu.VMEM((CHUNKS, GROUP, part, width), BF16),
            pltpu.VMEM((CHUNKS, GROUP, part, width), F32),
            pltpu.VMEM((CHUNKS, part, width), BF16),
            pltpu.VMEM((CHUNKS, 2, part, width), BF16),
            pltpu.VMEM((CHUNKS, width), F32),
            pltpu.VMEM((CHUNKS, width), F32),
            pltpu.VMEM((CHUNKS, GROUP, part, width), BF16),
            pltpu.VMEM((CHUNKS, GROUP, part, width), BF16),
            pltpu.VMEM((CHUNKS, nx, rows, width), BF16),
            pltpu.VMEM((CHUNKS, nx, rows, width), BF16),
            pltpu.VMEM((rows, channels), F32),
            pltpu.VMEM((rows, channels), F32),
            pltpu.VMEM((rows, channels), F32),
            pltpu.VMEM((rows, channels), F32),
            pltpu.VMEM((1, 128), F32),
            pltpu.VMEM((ntp, 1, 128), F32),
            sems((len(operands),)),
            sems((2,)),
            sems((2,)),
            sems((2,)),
            sems((2,)),
            sems((2,)),
            sems((CHUNKS, 2)),
            sems((CHUNKS, 2)),
            sems((CHUNKS, 4)),
            sems((2,)),
            sems((CHUNKS, 2)),
            sems((CHUNKS, 2)),
            sems((2,)),
            pltpu.SemaphoreType.REGULAR((3,)),
        ],
        compiler_params=pltpu.CompilerParams(
            collective_id=0, has_side_effects=True, vmem_limit_bytes=40 * 2**20
        ),
        cost_estimate=pl.CostEstimate(flops=2 * 10**8, bytes_accessed=2**20, transcendentals=10**6),
    )(*operands)


def solution(mesh):
    return jax.shard_map(
        per_device,
        mesh=mesh,
        in_specs=(
            P("seq", "tp"),
            P("seq", None, "tp"),
            P("seq", "tp"),
            P("seq", "tp"),
            P("seq"),
            P(None, "tp"),
            P(None, None, "tp"),
            P("tp"),
            P("tp"),
            P("tp"),
            P("tp"),
        ),
        out_specs=P("seq", "tp"),
        check_vma=False,
    )
```

```python
import functools

import jax
import jax.numpy as jnp
from jax import lax
from jax.experimental import pallas as pl
from jax.experimental.pallas import tpu as pltpu
from jax.sharding import PartitionSpec as P

NX = 4
GROUP = 4
CHUNKS = 2
HEAD = 16
REACH = 3
FOLD = 4
EPSILON = 1e-05
MESH = pl.DeviceIdType.MESH
F32, BF16 = jnp.float32, jnp.bfloat16


def dot(a, b):
    return jnp.dot(a, b, preferred_element_type=F32)


def dot_nt(a, b):
    return lax.dot_general(a, b, (((1,), (1,)), ((), ())), preferred_element_type=F32)


def dot_tn(a, b):
    return lax.dot_general(a, b, (((0,), (0,)), ((), ())), preferred_element_type=F32)


def iota(shape, axis):
    return lax.broadcasted_iota(jnp.int32, shape, axis)


def pieces(value, count):
    parts = []
    for _ in range(count):
        part = value.astype(BF16)
        parts.append(part)
        value = value - part.astype(F32)
    return jnp.concatenate(parts, axis=0)


def silu(value):
    return value * jax.nn.sigmoid(value)


def kernel(
    nz, nx, ntp,
    x_hbm, bc_hbm, z_hbm, dt_hbm, st_hbm, cx_hbm, cbc_hbm, al_hbm, db_hbm, ds_hbm, ng_hbm,
    out_ref,
    x_ref, bc_ref, z_ref, dt_ref, st_ref, cx_ref, cbc_ref, al_ref, db_ref, ds_ref, ng_ref,
    hsend, hrecv, pre, weights, xc, fx, bcv, crecv, dsend, drecv, tot_send, tot_recv,
    edge, erecv, sbuf, srecv, lbuf, ylbuf, tbuf, zrecv, prebuf, pout, pin, gsend, grecv, obuf, szbuf, ysend, yrecv,
    ebuf, yi, sz, gbuf, ssend, ssrecv,
    in_sem, h_sem, d_sem, t_sem, e_sem, c_sem, s_sem, zf_sem, p_sem, g_sem, zb_sem, y_sem, n_sem, near_sem,
):
    seq, tp = lax.axis_index("seq"), lax.axis_index("tp")
    mz, mx = seq // nx, seq % nx
    nseq, ngroups = nz * nx, nz // GROUP
    group, member = mz // GROUP, mz % GROUP
    rows, channels = x_ref.shape
    state = bc_ref.shape[2]
    heads = dt_ref.shape[0]
    quarter = channels // nx
    width = quarter // CHUNKS
    total_width = channels + 2 * state
    part = state // GROUP

    def seq_at(z, x):
        return {"seq": z * nx + x}

    def x_peer(r):
        q = (mx + r) % nx
        return q, seq_at(mz, q)

    def z_peer(r):
        k = (member + r) % GROUP
        return k, seq_at(group * GROUP + k, mx)

    def t_peer(r):
        return {"tp": (tp + r) % ntp}

    following, preceding = {"seq": seq + 1}, {"seq": seq - 1}
    swap = 1 - 2 * (member % 2)
    swapped = (group == ngroups - 1).astype(jnp.int32) * (ngroups > 2)
    to_swapped = (group == ngroups - 2).astype(jnp.int32) * (ngroups > 2)
    next_group = seq_at(mz + GROUP + to_swapped * swap, mx)

    def slice_of(k):
        return k + swapped * (1 - 2 * (k % 2))


    def remote(src, dst, sem, device):
        return pltpu.make_async_remote_copy(
            src_ref=src, dst_ref=dst, send_sem=sem.at[0], recv_sem=sem.at[1],
            device_id=device, device_id_type=MESH,
        )

    def await_recv(buffer, count, sem):
        some = buffer.at[pl.ds(0, count)]
        remote(some, some, sem, x_peer(1)[1]).wait_recv()

    def await_send(buffer, count, sem):
        some = buffer.at[pl.ds(0, count)]
        remote(some, some, sem, x_peer(1)[1]).wait_send()

    loads = [
        pltpu.make_async_copy(src, dst, in_sem.at[k])
        for k, (src, dst) in enumerate([
            (st_hbm, st_ref), (dt_hbm, dt_ref), (al_hbm, al_ref), (db_hbm, db_ref),
            (x_hbm, x_ref), (bc_hbm, bc_ref), (cx_hbm, cx_ref), (cbc_hbm, cbc_ref),
            (z_hbm, z_ref), (ds_hbm, ds_ref), (ng_hbm, ng_ref),
        ])
    ]
    for load in loads:
        load.start()

    barrier = pltpu.get_barrier_semaphore()

    def greet(device, sem=barrier):
        pl.semaphore_signal(sem, inc=1, device_id=device, device_id_type=MESH)

    for r in range(1, nx):
        greet(x_peer(r)[1])
    for r in range(1, GROUP):
        greet(z_peer(r)[1])

    first, last = member == 0, member == GROUP - 1
    below, above = group > 0, group + 1 < ngroups

    @pl.when(last & above)
    def _():
        greet(seq_at(mz + 1, mx))

    def greet_group(sem):
        for r in range(1, GROUP):
            greet(z_peer(r)[1], sem)

    @pl.when(seq > 0)
    def _():
        greet(preceding)

    for r in range(1, ntp):
        greet(t_peer(r))
    greeted = (nx - 1) + (GROUP - 1) + (ntp - 1)
    greeted += (seq + 1 < nseq).astype(jnp.int32) + (first & below).astype(jnp.int32)

    row, col = iota((rows, rows), 0), iota((rows, rows), 1)
    tril = (col <= row).astype(F32).astype(BF16)
    ranges = [tril, (col > row).astype(F32).astype(BF16)]
    for d in range(1, REACH + 1):
        ranges.append(((col <= row) & (col > row - d)).astype(F32).astype(BF16))
    spread = iota((heads, channels), 1) // (channels // heads) == iota((heads, channels), 0)
    spread = spread.astype(F32).astype(BF16)
    spread2 = jnp.concatenate([spread, spread], axis=0)
    for load in loads[:4]:
        load.wait()
    starts = jnp.broadcast_to(st_ref[...].astype(F32), (rows, rows)).astype(BF16)
    counts = dot_nt(jnp.concatenate(ranges, axis=0), starts)
    seg_col = counts[:rows]
    to_last = (counts[rows : 2 * rows] == 0.0).astype(F32)
    linked = (seg_col == dot_nt(starts, tril)) & (col <= row)
    from_first = (seg_col == 0.0).astype(F32)
    none_between = [counts[(d + 1) * rows : (d + 2) * rows] == 0.0 for d in range(1, REACH + 1)]
    taps = jnp.concatenate(
        [((col == row - d) & none_between[d - 1]).astype(F32).astype(BF16) for d in range(1, REACH + 1)],
        axis=0,
    )

    for load in loads[4:8]:
        load.wait()
    weights[:, :channels] = cx_ref[...]
    for k in range(REACH + 1):
        weights[k : k + 1, channels : channels + state] = cbc_ref[k, 0:1, :]
        weights[k : k + 1, channels + state :] = cbc_ref[k, 1:2, :]
    b_in, c_in = bc_ref[:, 0, :], bc_ref[:, 1, :]

    tail = slice(rows - 8, rows)
    last_rows = jnp.concatenate(
        [x_ref[tail, :].astype(F32), b_in[tail].astype(F32), c_in[tail].astype(F32)], axis=1
    )
    last_rows = (last_rows * to_last[tail, :1])[8 - FOLD :]
    piece = total_width // FOLD
    hsend[...] = jnp.concatenate(
        [last_rows[:, k * piece : (k + 1) * piece] for k in range(FOLD)], axis=0
    ).astype(BF16)

    def column(ref):
        square = (heads, heads)
        here = iota(square, 0) == iota(square, 1)
        return jnp.sum(jnp.where(here, jnp.broadcast_to(ref[...], square), 0.0), axis=1, keepdims=True)

    raw = dt_ref[...].astype(F32) + column(db_ref)
    step = jnp.maximum(raw, 0.0) + jnp.log1p(jnp.exp(-jnp.abs(raw)))
    decay = -jnp.exp(column(al_ref)) * step
    parts = dot_nt(pieces(decay, 3), tril)
    cumulative = parts[:heads] + parts[heads : 2 * heads] + parts[2 * heads :]
    ebuf[...] = dot_tn(pieces(jnp.exp(cumulative), 2), spread2)
    fall = ebuf[rows - 1 :, :]
    through = fall * (seg_col[rows - 1 : rows, :1] == 0.0).astype(F32)
    for q in range(nx):
        for c in range(CHUNKS):
            at = q * quarter + c * width
            dsend[q, c : c + 1, :] = through[:, at : at + width]
    factor = dot_tn(pieces(jnp.exp(-cumulative) * step, 2), spread2)

    def conv(values, at):
        size = values.shape[1]
        taken = weights[:, at : at + size]
        shifted = dot(taps, values)
        total = taken[REACH:] * values.astype(F32)
        for d in range(1, REACH + 1):
            total += taken[REACH - d : REACH - d + 1] * shifted[(d - 1) * rows : d * rows]
        pre[:, at : at + size] = total[:HEAD]
        return silu(total)

    bcv[:, :state] = conv(b_in, channels).astype(BF16)
    bcv[:, state:] = conv(c_in, channels + state).astype(BF16)
    for at in range(0, channels, 256):
        xc[:, at : at + 256] = conv(x_ref[:, at : at + 256], at).astype(BF16)

    for at in range(0, channels, 256):
        at = slice(at, at + 256)
        fx[:, at] = (xc[:, at].astype(F32) * factor[:, at]).astype(BF16)
    later = to_last * (row >= HEAD).astype(F32)
    bt = jnp.transpose(bcv[:, :state].astype(F32) * later[:, :1]).astype(BF16)
    for c in range(CHUNKS):
        for q in range(nx):
            at = slice(q * quarter + c * width, q * quarter + (c + 1) * width)
            sbuf[c, q] = (dot(bt, fx[:, at]) * fall[:, at]).astype(BF16)

    place_row, place_col = iota((HEAD, HEAD), 0), iota((HEAD, HEAD), 1)
    reached = []
    for k in range(FOLD):
        matrices = []
        for d in range(1, REACH + 1):
            here = (place_col - (k + 1) * FOLD == place_row - d) & (place_row < d)
            here &= none_between[d - 1][:HEAD, :HEAD] & (place_col >= k * FOLD)
            matrices.append(here.astype(F32).astype(BF16))
        reached.append(jnp.concatenate(matrices, axis=0))

    pl.semaphore_wait(barrier, greeted)

    halo = remote(hsend, hrecv, h_sem, following)

    @pl.when(seq + 1 < nseq)
    def _():
        halo.start()

    @pl.when(first & below)
    def _():
        greet(seq_at(mz - 1, mx), near_sem.at[0])

    for r in range(1, nx):
        q, device = x_peer(r)
        remote(dsend.at[q], drecv.at[mx], d_sem, device).start()
    def send_states(c):
        for r in (2, 1, 3) if nx == 4 else range(1, nx):
            q, device = x_peer(r)
            remote(sbuf.at[c, q], srecv.at[c, mx], s_sem.at[c], device).start()

    send_states(0)
    drecv[mx] = dsend[mx]
    for c in range(CHUNKS):
        srecv[c, mx] = sbuf[c, mx]

    @pl.when(seq == 0)
    def _():
        hrecv[...] = jnp.zeros(hrecv.shape, BF16)

    @pl.when(seq > 0)
    def _():
        halo.wait_recv()

    for k in range(FOLD):
        at = slice(k * piece, (k + 1) * piece)
        added = dot(reached[k], hrecv[...])
        total = pre[:, at]
        for d in range(1, REACH + 1):
            total += weights[REACH - d : REACH - d + 1, at] * added[(d - 1) * HEAD : d * HEAD]
        pre[:, at] = total
    done = silu(pre[...]).astype(BF16)
    xc[:HEAD, :] = done[:, :channels]
    bcv[:HEAD, :] = done[:, channels:]
    first_x = done[:, :channels].astype(F32) * factor[:HEAD]
    fx[:HEAD, :] = first_x.astype(BF16)
    first_x = (first_x * fall).astype(BF16)
    first_b = (done[:, channels : channels + state].astype(F32) * to_last[:HEAD, :1]).astype(BF16)
    for q in range(nx):
        edge[q, :, :state] = first_b
        edge[q, :, state:] = first_x[:, q * quarter : (q + 1) * quarter]
    erecv[mx] = edge[mx]
    for r in range(1, nx):
        q, device = x_peer(r)
        remote(edge.at[q], erecv.at[mx], e_sem, device).start()
    for c in range(1, CHUNKS):
        send_states(c)
    b, cc = bcv[:, :state], bcv[:, state:]
    crecv[mx] = cc

    await_recv(drecv, nx - 1, d_sem)
    reach_of = [None, drecv[0]]
    for k in range(1, nx):
        reach_of.append(reach_of[-1] * drecv[k])
    tot_send[...] = reach_of[nx]
    tot_recv[member] = reach_of[nx]
    for r in range(1, GROUP):
        k, device = z_peer(r)
        remote(tot_send, tot_recv.at[member], t_sem, device).start()
    @pl.when(last & above)
    def _():
        pl.semaphore_wait(near_sem.at[0], 1)
        greet_group(near_sem.at[1])

    scores = jnp.where(linked, dot_nt(cc, b), 0.0).astype(BF16)
    for load in loads[8:]:
        load.wait()
    skip = dot_tn(pieces(jnp.broadcast_to(column(ds_ref), (heads, 128)), 2), spread2)[:1]
    for q in range(nx):
        at = slice(q * quarter, (q + 1) * quarter)
        gate = silu(z_ref[:, at].astype(F32))
        own = ebuf[:, at] * dot(scores, fx[:, at]) + skip[:, at] * xc[:, at].astype(F32)
        yi[:, at] = own * gate
        sz[:, at] = ebuf[:, at] * from_first[:, :1] * gate

    await_recv(erecv, nx - 1, e_sem)

    def made(c, k):
        first = dot_tn(erecv[k, :, :state], erecv[k, :, state + c * width : state + (c + 1) * width])
        return srecv[c, k].astype(F32) + first

    for c in range(CHUNKS):
        await_recv(srecv.at[c], nx - 1, s_sem.at[c])
        running = made(c, 0)
        for k in range(1, nx):
            lbuf[c, k - 1] = running.astype(BF16)
            running = drecv[k, c : c + 1, :] * running + made(c, k)
        tbuf[c] = running.astype(BF16).reshape(GROUP, part, width)
        zrecv[c, member] = tbuf[c, slice_of(member)]
        for r in range(1, GROUP):
            k, device = z_peer(r)
            remote(tbuf.at[c, slice_of(k)], zrecv.at[c, member], zf_sem.at[c], device).start()

    for r in range(1, nx):
        _, device = x_peer(r)
        remote(crecv.at[mx], crecv.at[mx], c_sem, device).start()

    @pl.when(jnp.logical_not(last) & above)
    def _():
        pl.semaphore_wait(near_sem.at[1], 1)

    if ngroups > 2:
        @pl.when(first & (group == 2))
        def _():
            greet(seq_at(mz - 1, mx), near_sem.at[2])

        @pl.when(last & (group == 1))
        def _():
            pl.semaphore_wait(near_sem.at[2], 1)
            greet_group(near_sem.at[3])

    await_recv(tot_recv, GROUP - 1, t_sem)
    row_fall = [tot_recv[k] for k in range(GROUP)]
    group_fall = row_fall[0]
    for k in range(1, GROUP):
        group_fall = row_fall[k] * group_fall
    even = group % 2 == 0
    share_decay = remote(gsend, grecv, g_sem, next_group)

    def hand_on(c, slot, device, sent=0):
        return pltpu.make_async_remote_copy(
            src_ref=pout.at[c], dst_ref=pin.at[c, slot],
            send_sem=p_sem.at[c, sent], recv_sem=p_sem.at[c, 2 + slot],
            device_id=device, device_id_type=MESH,
        )

    after_next_group = seq_at(mz + 2 * GROUP + swap, mx)

    @pl.when(even)
    def _():
        gsend[...] = group_fall
        share_decay.start()
        grecv[...] = jnp.ones(grecv.shape, F32)
        pin[:, 0] = jnp.zeros((CHUNKS, part, width), BF16)

    @pl.when(group < 2)
    def _():
        pin[:, 1] = jnp.zeros((CHUNKS, part, width), BF16)

    group_totals = []
    for c in range(CHUNKS):
        await_recv(zrecv.at[c], GROUP - 1, zf_sem.at[c])
        running = zrecv[c, 0].astype(F32)
        for k in range(1, GROUP):
            prebuf[c, k] = running
            running = row_fall[k][c : c + 1] * running + zrecv[c, k].astype(F32)
        group_totals.append(running)

        @pl.when(even)
        def _():
            pout[c] = running.astype(BF16)
            hand_on(c, 0, next_group).start()

    @pl.when(jnp.logical_not(even))
    def _():
        share_decay.wait_recv()
        for c in range(CHUNKS):
            hand_on(c, 0, next_group).wait_recv()

    if ngroups > 2:
        @pl.when(group == 1)
        def _():
            @pl.when(jnp.logical_not(last))
            def _():
                pl.semaphore_wait(near_sem.at[3], 1)

            for c in range(CHUNKS):
                reached = group_fall[c : c + 1] * pin[c, 0].astype(F32) + group_totals[c]
                pout[c] = reached.astype(BF16)
                hand_on(c, 1, after_next_group, 1).start()
                hand_on(c, 1, next_group).start()

    for c in range(CHUNKS):
        if ngroups > 2:
            @pl.when(group >= 2)
            def _():
                hand_on(c, 1, next_group).wait_recv()

        before = grecv[c : c + 1] * pin[c, 1].astype(F32) + pin[c, 0].astype(F32)
        obuf[c, 0] = before.astype(BF16)
        reach = row_fall[0][c : c + 1]
        for k in range(1, GROUP):
            obuf[c, k] = (reach * before + prebuf[c, k]).astype(BF16)
            reach = row_fall[k][c : c + 1] * reach
        szbuf[c, slice_of(member)] = obuf[c, member]
        for r in range(1, GROUP):
            k, device = z_peer(r)
            remote(obuf.at[c, k], szbuf.at[c, slice_of(member)], zb_sem.at[c], device).start()

    await_recv(crecv, nx - 1, c_sem)
    for c in range(CHUNKS):
        for k in range(1, nx):
            ylbuf[c, k - 1] = dot(crecv[k], lbuf[c, k - 1])

    for c in range(CHUNKS):
        await_recv(szbuf.at[c], GROUP - 1, zb_sem.at[c])
        entering = szbuf[c].reshape(state, width)
        for k in range(nx):
            part_y = dot(crecv[k], entering)
            if k:
                part_y = reach_of[k][c : c + 1, :] * part_y + ylbuf[c, k - 1]
            ysend[c, k] = part_y.astype(BF16)
        yrecv[c, mx] = ysend[c, mx]
        for r in range(1, nx):
            q, device = x_peer(r)
            remote(ysend.at[c, q], yrecv.at[c, mx], y_sem.at[c], device).start()

    squares = jnp.zeros((rows, 128), F32)
    for c in range(CHUNKS):
        await_recv(yrecv.at[c], nx - 1, y_sem.at[c])
        for q in range(nx):
            at = slice(q * quarter + c * width, q * quarter + (c + 1) * width)
            gated = yi[:, at] + sz[:, at] * yrecv[c, q].astype(F32)
            gbuf[:, at] = gated
            for k in range(0, width, 128):
                some = gated[:, k : k + 128]
                squares += some * some
    total = jnp.sum(jnp.transpose(squares), axis=0, keepdims=True)
    total = jnp.broadcast_to(total, ssend.shape)
    ssend[...] = total
    ssrecv[tp] = total
    for r in range(1, ntp):
        remote(ssend, ssrecv.at[tp], n_sem, t_peer(r)).start()
    await_recv(ssrecv, ntp - 1, n_sem)
    total = jnp.sum(ssrecv[...], axis=0)[:1]
    inverse = lax.rsqrt(total / (channels * ntp) + EPSILON)
    inverse = jnp.transpose(jnp.broadcast_to(inverse, (rows, rows)))
    for at in range(0, channels, 128):
        at = slice(at, at + 128)
        out_ref[:, at] = (gbuf[:, at] * inverse * ng_ref[:, at]).astype(BF16)

    @pl.when(seq + 1 < nseq)
    def _():
        halo.wait_send()

    await_send(drecv, nx - 1, d_sem)
    await_send(tot_recv, GROUP - 1, t_sem)
    await_send(erecv, nx - 1, e_sem)
    await_send(crecv, nx - 1, c_sem)
    for c in range(CHUNKS):
        await_send(srecv.at[c], nx - 1, s_sem.at[c])
        await_send(zrecv.at[c], GROUP - 1, zf_sem.at[c])

        @pl.when(even)
        def _():
            if c == 0:
                share_decay.wait_send()
            hand_on(c, 0, next_group).wait_send()

        if ngroups > 2:
            @pl.when(group == 1)
            def _():
                hand_on(c, 1, next_group).wait_send()
                hand_on(c, 1, after_next_group, 1).wait_send()

        await_send(szbuf.at[c], GROUP - 1, zb_sem.at[c])
        await_send(yrecv.at[c], nx - 1, y_sem.at[c])
    await_send(ssrecv, ntp - 1, n_sem)


def per_device(
    x_in, bc_in, z_in, dt_raw, starts, conv_x, conv_bc, a_log, dt_bias, d_skip, norm_gain
):
    rows, channels = x_in.shape
    state = bc_in.shape[2]
    heads = dt_raw.shape[1]
    nx, ntp = NX, lax.axis_size("tp")
    nz = lax.axis_size("seq") // nx
    width = channels // nx // CHUNKS
    total_width = channels + 2 * state
    part = state // GROUP
    operands = (
        x_in,
        bc_in,
        z_in,
        dt_raw.T,
        starts.reshape(1, rows),
        conv_x,
        conv_bc,
        a_log.reshape(1, heads),
        dt_bias.reshape(1, heads),
        d_skip.reshape(1, heads),
        norm_gain.reshape(1, channels),
    )
    operands = tuple(pltpu.with_memory_space_constraint(o, pltpu.HBM) for o in operands)
    sems = pltpu.SemaphoreType.DMA
    return pl.pallas_call(
        functools.partial(kernel, nz, nx, ntp),
        out_shape=jax.ShapeDtypeStruct((rows, channels), BF16),
        in_specs=[pl.BlockSpec(memory_space=pltpu.HBM)] * len(operands),
        out_specs=pl.BlockSpec(memory_space=pltpu.VMEM),
        scratch_shapes=[
            *(pltpu.VMEM(operand.shape, operand.dtype) for operand in operands),
            pltpu.VMEM((4 * FOLD, total_width // FOLD), BF16),
            pltpu.VMEM((4 * FOLD, total_width // FOLD), BF16),
            pltpu.VMEM((HEAD, total_width), F32),
            pltpu.VMEM((REACH + 1, total_width), F32),
            pltpu.VMEM((rows, channels), BF16),
            pltpu.VMEM((rows, channels), BF16),
            pltpu.VMEM((rows, 2 * state), BF16),
            pltpu.VMEM((nx, rows, state), BF16),
            pltpu.VMEM((nx, CHUNKS, width), F32),
            pltpu.VMEM((nx, CHUNKS, width), F32),
            pltpu.VMEM((CHUNKS, width), F32),
            pltpu.VMEM((GROUP, CHUNKS, width), F32),
            pltpu.VMEM((nx, HEAD, state + width * CHUNKS), BF16),
            pltpu.VMEM((nx, HEAD, state + width * CHUNKS), BF16),
            pltpu.VMEM((CHUNKS, nx, state, width), BF16),
            pltpu.VMEM((CHUNKS, nx, state, width), BF16),
            pltpu.VMEM((CHUNKS, nx - 1, state, width), BF16),
            pltpu.VMEM((CHUNKS, nx - 1, rows, width), F32),
            pltpu.VMEM((CHUNKS, GROUP, part, width), BF16),
            pltpu.VMEM((CHUNKS, GROUP, part, width), BF16),
            pltpu.VMEM((CHUNKS, GROUP, part, width), F32),
            pltpu.VMEM((CHUNKS, part, width), BF16),
            pltpu.VMEM((CHUNKS, 2, part, width), BF16),
            pltpu.VMEM((CHUNKS, width), F32),
            pltpu.VMEM((CHUNKS, width), F32),
            pltpu.VMEM((CHUNKS, GROUP, part, width), BF16),
            pltpu.VMEM((CHUNKS, GROUP, part, width), BF16),
            pltpu.VMEM((CHUNKS, nx, rows, width), BF16),
            pltpu.VMEM((CHUNKS, nx, rows, width), BF16),
            pltpu.VMEM((rows, channels), F32),
            pltpu.VMEM((rows, channels), F32),
            pltpu.VMEM((rows, channels), F32),
            pltpu.VMEM((rows, channels), F32),
            pltpu.VMEM((1, 128), F32),
            pltpu.VMEM((ntp, 1, 128), F32),
            sems((len(operands),)),
            sems((2,)),
            sems((2,)),
            sems((2,)),
            sems((2,)),
            sems((2,)),
            sems((CHUNKS, 2)),
            sems((CHUNKS, 2)),
            sems((CHUNKS, 4)),
            sems((2,)),
            sems((CHUNKS, 2)),
            sems((CHUNKS, 2)),
            sems((2,)),
            pltpu.SemaphoreType.REGULAR((4,)),
        ],
        compiler_params=pltpu.CompilerParams(
            collective_id=0, has_side_effects=True, vmem_limit_bytes=40 * 2**20
        ),
        cost_estimate=pl.CostEstimate(flops=2 * 10**8, bytes_accessed=2**20, transcendentals=10**6),
    )(*operands)


def solution(mesh):
    return jax.shard_map(
        per_device,
        mesh=mesh,
        in_specs=(
            P("seq", "tp"),
            P("seq", None, "tp"),
            P("seq", "tp"),
            P("seq", "tp"),
            P("seq"),
            P(None, "tp"),
            P(None, None, "tp"),
            P("tp"),
            P("tp"),
            P("tp"),
            P("tp"),
        ),
        out_specs=P("seq", "tp"),
        check_vma=False,
    )
```

```python
import functools

import jax
import jax.numpy as jnp
from jax import lax
from jax.experimental import pallas as pl
from jax.experimental.pallas import tpu as pltpu
from jax.sharding import PartitionSpec as P

NX = 4
GROUP = 4
CHUNKS = 2
HEAD = 16
REACH = 3
FOLD = 4
EPSILON = 1e-05
MESH = pl.DeviceIdType.MESH
F32, BF16 = jnp.float32, jnp.bfloat16


def dot(a, b):
    return jnp.dot(a, b, preferred_element_type=F32)


def dot_nt(a, b):
    return lax.dot_general(a, b, (((1,), (1,)), ((), ())), preferred_element_type=F32)


def dot_tn(a, b):
    return lax.dot_general(a, b, (((0,), (0,)), ((), ())), preferred_element_type=F32)


def iota(shape, axis):
    return lax.broadcasted_iota(jnp.int32, shape, axis)


def pieces(value, count):
    parts = []
    for _ in range(count):
        part = value.astype(BF16)
        parts.append(part)
        value = value - part.astype(F32)
    return jnp.concatenate(parts, axis=0)


def silu(value):
    return value * jax.nn.sigmoid(value)


def kernel(
    nz, nx, ntp,
    x_hbm, bc_hbm, z_hbm, dt_hbm, st_hbm, cx_hbm, cbc_hbm, al_hbm, db_hbm, ds_hbm, ng_hbm,
    out_ref,
    x_ref, bc_ref, z_ref, dt_ref, st_ref, cx_ref, cbc_ref, al_ref, db_ref, ds_ref, ng_ref,
    hsend, hrecv, pre, weights, xc, fx, bcv, crecv, dsend, drecv, tot_send, tot_recv,
    edge, erecv, sbuf, srecv, lbuf, ylbuf, tbuf, zrecv, prebuf, pout, pin, gsend, grecv, obuf, szbuf, ysend, yrecv,
    ebuf, yi, sz, gbuf, ssend, ssrecv,
    in_sem, h_sem, d_sem, t_sem, e_sem, c_sem, s_sem, zf_sem, p_sem, g_sem, zb_sem, y_sem, n_sem, near_sem,
):
    seq, tp = lax.axis_index("seq"), lax.axis_index("tp")
    mz, mx = seq // nx, seq % nx
    nseq, ngroups = nz * nx, nz // GROUP
    group, member = mz // GROUP, mz % GROUP
    rows, channels = x_ref.shape
    state = bc_ref.shape[2]
    heads = dt_ref.shape[0]
    quarter = channels // nx
    width = quarter // CHUNKS
    total_width = channels + 2 * state
    part = state // GROUP

    def seq_at(z, x):
        return {"seq": z * nx + x}

    def x_peer(r):
        q = (mx + r) % nx
        return q, seq_at(mz, q)

    def z_peer(r):
        k = (member + r) % GROUP
        return k, seq_at(group * GROUP + k, mx)

    def t_peer(r):
        return {"tp": (tp + r) % ntp}

    following, preceding = {"seq": seq + 1}, {"seq": seq - 1}
    swap = 1 - 2 * (member % 2)
    swapped = (group == ngroups - 1).astype(jnp.int32) * (ngroups > 2)
    to_swapped = (group == ngroups - 2).astype(jnp.int32) * (ngroups > 2)
    next_group = seq_at(mz + GROUP + to_swapped * swap, mx)

    def slice_of(k):
        return k + swapped * (1 - 2 * (k % 2))


    def remote(src, dst, sem, device):
        return pltpu.make_async_remote_copy(
            src_ref=src, dst_ref=dst, send_sem=sem.at[0], recv_sem=sem.at[1],
            device_id=device, device_id_type=MESH,
        )

    def await_recv(buffer, count, sem):
        some = buffer.at[pl.ds(0, count)]
        remote(some, some, sem, x_peer(1)[1]).wait_recv()

    def await_send(buffer, count, sem):
        some = buffer.at[pl.ds(0, count)]
        remote(some, some, sem, x_peer(1)[1]).wait_send()

    loads = [
        pltpu.make_async_copy(src, dst, in_sem.at[k])
        for k, (src, dst) in enumerate([
            (st_hbm, st_ref), (dt_hbm, dt_ref), (al_hbm, al_ref), (db_hbm, db_ref),
            (x_hbm, x_ref), (bc_hbm, bc_ref), (cx_hbm, cx_ref), (cbc_hbm, cbc_ref),
            (z_hbm, z_ref), (ds_hbm, ds_ref), (ng_hbm, ng_ref),
        ])
    ]
    for load in loads:
        load.start()

    barrier = pltpu.get_barrier_semaphore()

    def greet(device, sem=barrier):
        pl.semaphore_signal(sem, inc=1, device_id=device, device_id_type=MESH)

    for r in range(1, nx):
        greet(x_peer(r)[1])
    for r in range(1, GROUP):
        greet(z_peer(r)[1])

    first, last = member == 0, member == GROUP - 1
    below, above = group > 0, group + 1 < ngroups

    @pl.when(last & above)
    def _():
        greet(seq_at(mz + 1, mx))

    def greet_group(sem):
        for r in range(1, GROUP):
            greet(z_peer(r)[1], sem)

    @pl.when(seq > 0)
    def _():
        greet(preceding)

    for r in range(1, ntp):
        greet(t_peer(r))
    greeted = (nx - 1) + (GROUP - 1) + (ntp - 1)
    greeted += (seq + 1 < nseq).astype(jnp.int32) + (first & below).astype(jnp.int32)

    row, col = iota((rows, rows), 0), iota((rows, rows), 1)
    tril = (col <= row).astype(F32).astype(BF16)
    ranges = [tril, (col > row).astype(F32).astype(BF16)]
    for d in range(1, REACH + 1):
        ranges.append(((col <= row) & (col > row - d)).astype(F32).astype(BF16))
    spread = iota((heads, channels), 1) // (channels // heads) == iota((heads, channels), 0)
    spread = spread.astype(F32).astype(BF16)
    spread2 = jnp.concatenate([spread, spread], axis=0)
    for load in loads[:4]:
        load.wait()
    starts = jnp.broadcast_to(st_ref[...].astype(F32), (rows, rows)).astype(BF16)
    counts = dot_nt(jnp.concatenate(ranges, axis=0), starts)
    seg_col = counts[:rows]
    to_last = (counts[rows : 2 * rows] == 0.0).astype(F32)
    linked = (seg_col == dot_nt(starts, tril)) & (col <= row)
    from_first = (seg_col == 0.0).astype(F32)
    none_between = [counts[(d + 1) * rows : (d + 2) * rows] == 0.0 for d in range(1, REACH + 1)]
    taps = jnp.concatenate(
        [((col == row - d) & none_between[d - 1]).astype(F32).astype(BF16) for d in range(1, REACH + 1)],
        axis=0,
    )

    for load in loads[4:8]:
        load.wait()
    weights[:, :channels] = cx_ref[...]
    for k in range(REACH + 1):
        weights[k : k + 1, channels : channels + state] = cbc_ref[k, 0:1, :]
        weights[k : k + 1, channels + state :] = cbc_ref[k, 1:2, :]
    b_in, c_in = bc_ref[:, 0, :], bc_ref[:, 1, :]

    tail = slice(rows - 8, rows)
    last_rows = jnp.concatenate(
        [x_ref[tail, :].astype(F32), b_in[tail].astype(F32), c_in[tail].astype(F32)], axis=1
    )
    last_rows = (last_rows * to_last[tail, :1])[8 - FOLD :]
    piece = total_width // FOLD
    hsend[...] = jnp.concatenate(
        [last_rows[:, k * piece : (k + 1) * piece] for k in range(FOLD)], axis=0
    ).astype(BF16)

    def column(ref):
        square = (heads, heads)
        here = iota(square, 0) == iota(square, 1)
        return jnp.sum(jnp.where(here, jnp.broadcast_to(ref[...], square), 0.0), axis=1, keepdims=True)

    raw = dt_ref[...].astype(F32) + column(db_ref)
    step = jnp.maximum(raw, 0.0) + jnp.log1p(jnp.exp(-jnp.abs(raw)))
    decay = -jnp.exp(column(al_ref)) * step
    parts = dot_nt(pieces(decay, 3), tril)
    cumulative = parts[:heads] + parts[heads : 2 * heads] + parts[2 * heads :]
    ebuf[...] = dot_tn(pieces(jnp.exp(cumulative), 2), spread2)
    fall = ebuf[rows - 1 :, :]
    through = fall * (seg_col[rows - 1 : rows, :1] == 0.0).astype(F32)
    for q in range(nx):
        for c in range(CHUNKS):
            at = q * quarter + c * width
            dsend[q, c : c + 1, :] = through[:, at : at + width]
    factor = dot_tn(pieces(jnp.exp(-cumulative) * step, 2), spread2)

    def conv(values, at):
        size = values.shape[1]
        taken = weights[:, at : at + size]
        shifted = dot(taps, values)
        total = taken[REACH:] * values.astype(F32)
        for d in range(1, REACH + 1):
            total += taken[REACH - d : REACH - d + 1] * shifted[(d - 1) * rows : d * rows]
        pre[:, at : at + size] = total[:HEAD]
        return silu(total)

    bcv[:, :state] = conv(b_in, channels).astype(BF16)
    bcv[:, state:] = conv(c_in, channels + state).astype(BF16)
    for at in range(0, channels, 256):
        xc[:, at : at + 256] = conv(x_ref[:, at : at + 256], at).astype(BF16)

    for at in range(0, channels, 256):
        at = slice(at, at + 256)
        fx[:, at] = (xc[:, at].astype(F32) * factor[:, at]).astype(BF16)
    later = to_last * (row >= HEAD).astype(F32)
    bt = jnp.transpose(bcv[:, :state].astype(F32) * later[:, :1]).astype(BF16)
    for c in range(CHUNKS):
        for q in range(nx):
            at = slice(q * quarter + c * width, q * quarter + (c + 1) * width)
            sbuf[c, q] = (dot(bt, fx[:, at]) * fall[:, at]).astype(BF16)

    place_row, place_col = iota((HEAD, HEAD), 0), iota((HEAD, HEAD), 1)
    reached = []
    for k in range(FOLD):
        matrices = []
        for d in range(1, REACH + 1):
            here = (place_col - (k + 1) * FOLD == place_row - d) & (place_row < d)
            here &= none_between[d - 1][:HEAD, :HEAD] & (place_col >= k * FOLD)
            matrices.append(here.astype(F32).astype(BF16))
        reached.append(jnp.concatenate(matrices, axis=0))

    pl.semaphore_wait(barrier, greeted)

    halo = remote(hsend, hrecv, h_sem, following)

    @pl.when(seq + 1 < nseq)
    def _():
        halo.start()

    @pl.when(first & below)
    def _():
        greet(seq_at(mz - 1, mx), near_sem.at[0])

    for r in range(1, nx):
        q, device = x_peer(r)
        remote(dsend.at[q], drecv.at[mx], d_sem, device).start()
    def send_states(c):
        for r in (2, 1, 3) if nx == 4 else range(1, nx):
            q, device = x_peer(r)
            remote(sbuf.at[c, q], srecv.at[c, mx], s_sem.at[c], device).start()

    send_states(0)
    drecv[mx] = dsend[mx]
    for c in range(CHUNKS):
        srecv[c, mx] = sbuf[c, mx]

    @pl.when(seq == 0)
    def _():
        hrecv[...] = jnp.zeros(hrecv.shape, BF16)

    @pl.when(seq > 0)
    def _():
        halo.wait_recv()

    for k in range(FOLD):
        at = slice(k * piece, (k + 1) * piece)
        added = dot(reached[k], hrecv[...])
        total = pre[:, at]
        for d in range(1, REACH + 1):
            total += weights[REACH - d : REACH - d + 1, at] * added[(d - 1) * HEAD : d * HEAD]
        pre[:, at] = total
    done = silu(pre[...]).astype(BF16)
    xc[:HEAD, :] = done[:, :channels]
    bcv[:HEAD, :] = done[:, channels:]
    first_x = done[:, :channels].astype(F32) * factor[:HEAD]
    fx[:HEAD, :] = first_x.astype(BF16)
    first_x = (first_x * fall).astype(BF16)
    first_b = (done[:, channels : channels + state].astype(F32) * to_last[:HEAD, :1]).astype(BF16)
    for q in range(nx):
        edge[q, :, :state] = first_b
        edge[q, :, state:] = first_x[:, q * quarter : (q + 1) * quarter]
    erecv[mx] = edge[mx]
    for r in range(1, nx):
        q, device = x_peer(r)
        remote(edge.at[q], erecv.at[mx], e_sem, device).start()
    for c in range(1, CHUNKS):
        send_states(c)
    b, cc = bcv[:, :state], bcv[:, state:]
    crecv[mx] = cc

    await_recv(drecv, nx - 1, d_sem)
    reach_of = [None, drecv[0]]
    for k in range(1, nx):
        reach_of.append(reach_of[-1] * drecv[k])
    tot_send[...] = reach_of[nx]
    tot_recv[member] = reach_of[nx]
    for r in range(1, GROUP):
        k, device = z_peer(r)
        remote(tot_send, tot_recv.at[member], t_sem, device).start()
    @pl.when(last & above)
    def _():
        pl.semaphore_wait(near_sem.at[0], 1)
        greet_group(near_sem.at[1])

    scores = jnp.where(linked, dot_nt(cc, b), 0.0).astype(BF16)
    for load in loads[8:]:
        load.wait()
    skip = dot_tn(pieces(jnp.broadcast_to(column(ds_ref), (heads, 128)), 2), spread2)[:1]
    for q in range(nx):
        at = slice(q * quarter, (q + 1) * quarter)
        gate = silu(z_ref[:, at].astype(F32))
        own = ebuf[:, at] * dot(scores, fx[:, at]) + skip[:, at] * xc[:, at].astype(F32)
        yi[:, at] = own * gate
        sz[:, at] = ebuf[:, at] * from_first[:, :1] * gate

    await_recv(erecv, nx - 1, e_sem)

    def made(c, k):
        first = dot_tn(erecv[k, :, :state], erecv[k, :, state + c * width : state + (c + 1) * width])
        return srecv[c, k].astype(F32) + first

    for c in range(CHUNKS):
        await_recv(srecv.at[c], nx - 1, s_sem.at[c])
        running = made(c, 0)
        for k in range(1, nx):
            lbuf[c, k - 1] = running.astype(BF16)
            running = drecv[k, c : c + 1, :] * running + made(c, k)
        tbuf[c] = running.astype(BF16).reshape(GROUP, part, width)
        zrecv[c, member] = tbuf[c, slice_of(member)]
        for r in range(1, GROUP):
            k, device = z_peer(r)
            remote(tbuf.at[c, slice_of(k)], zrecv.at[c, member], zf_sem.at[c], device).start()

    for r in range(1, nx):
        _, device = x_peer(r)
        remote(crecv.at[mx], crecv.at[mx], c_sem, device).start()

    @pl.when(jnp.logical_not(last) & above)
    def _():
        pl.semaphore_wait(near_sem.at[1], 1)

    if ngroups > 2:
        @pl.when(first & (group == 2))
        def _():
            greet(seq_at(mz - 1, mx), near_sem.at[2])

        @pl.when(last & (group == 1))
        def _():
            pl.semaphore_wait(near_sem.at[2], 1)
            greet_group(near_sem.at[3])

    await_recv(tot_recv, GROUP - 1, t_sem)
    row_fall = [tot_recv[k] for k in range(GROUP)]
    group_fall = row_fall[0]
    for k in range(1, GROUP):
        group_fall = row_fall[k] * group_fall
    even = group % 2 == 0
    share_decay = remote(gsend, grecv, g_sem, next_group)

    def hand_on(c, slot, device, sent=0):
        return pltpu.make_async_remote_copy(
            src_ref=pout.at[c], dst_ref=pin.at[c, slot],
            send_sem=p_sem.at[c, sent], recv_sem=p_sem.at[c, 2 + slot],
            device_id=device, device_id_type=MESH,
        )

    after_next_group = seq_at(mz + 2 * GROUP + swap, mx)

    @pl.when(even)
    def _():
        gsend[...] = group_fall
        share_decay.start()
        grecv[...] = jnp.ones(grecv.shape, F32)
        pin[:, 0] = jnp.zeros((CHUNKS, part, width), BF16)

    @pl.when(group < 2)
    def _():
        pin[:, 1] = jnp.zeros((CHUNKS, part, width), BF16)

    for c in range(CHUNKS):
        await_recv(zrecv.at[c], GROUP - 1, zf_sem.at[c])
        running = zrecv[c, 0].astype(F32)
        for k in range(1, GROUP):
            prebuf[c, k] = running
            running = row_fall[k][c : c + 1] * running + zrecv[c, k].astype(F32)

        @pl.when(even)
        def _():
            pout[c] = running.astype(BF16)
            hand_on(c, 0, next_group).start()

        if ngroups > 2:
            @pl.when(group == 1)
            def _():
                if c == 0:
                    @pl.when(jnp.logical_not(last))
                    def _():
                        pl.semaphore_wait(near_sem.at[3], 1)

                hand_on(c, 0, next_group).wait_recv()
                reached = group_fall[c : c + 1] * pin[c, 0].astype(F32) + running
                pout[c] = reached.astype(BF16)
                hand_on(c, 1, after_next_group, 1).start()
                hand_on(c, 1, next_group).start()

    @pl.when(jnp.logical_not(even))
    def _():
        share_decay.wait_recv()

    for c in range(CHUNKS):
        @pl.when(jnp.logical_not(even) & ((group != 1) | (ngroups <= 2)))
        def _():
            hand_on(c, 0, next_group).wait_recv()

        if ngroups > 2:
            @pl.when(group >= 2)
            def _():
                hand_on(c, 1, next_group).wait_recv()

        before = grecv[c : c + 1] * pin[c, 1].astype(F32) + pin[c, 0].astype(F32)
        obuf[c, 0] = before.astype(BF16)
        reach = row_fall[0][c : c + 1]
        for k in range(1, GROUP):
            obuf[c, k] = (reach * before + prebuf[c, k]).astype(BF16)
            reach = row_fall[k][c : c + 1] * reach
        szbuf[c, slice_of(member)] = obuf[c, member]
        for r in range(1, GROUP):
            k, device = z_peer(r)
            remote(obuf.at[c, k], szbuf.at[c, slice_of(member)], zb_sem.at[c], device).start()

    await_recv(crecv, nx - 1, c_sem)
    for c in range(CHUNKS):
        for k in range(1, nx):
            ylbuf[c, k - 1] = dot(crecv[k], lbuf[c, k - 1])

    for c in range(CHUNKS):
        await_recv(szbuf.at[c], GROUP - 1, zb_sem.at[c])
        entering = szbuf[c].reshape(state, width)
        all_y = dot(crecv[...].reshape(nx * rows, state), entering)
        for k in range(nx):
            part_y = all_y[k * rows : (k + 1) * rows]
            if k:
                part_y = reach_of[k][c : c + 1, :] * part_y + ylbuf[c, k - 1]
            ysend[c, k] = part_y.astype(BF16)
        yrecv[c, mx] = ysend[c, mx]
        for r in range(1, nx):
            q, device = x_peer(r)
            remote(ysend.at[c, q], yrecv.at[c, mx], y_sem.at[c], device).start()

    squares = jnp.zeros((rows, 128), F32)
    for c in range(CHUNKS):
        await_recv(yrecv.at[c], nx - 1, y_sem.at[c])
        for q in range(nx):
            at = slice(q * quarter + c * width, q * quarter + (c + 1) * width)
            gated = yi[:, at] + sz[:, at] * yrecv[c, q].astype(F32)
            gbuf[:, at] = gated
            for k in range(0, width, 128):
                some = gated[:, k : k + 128]
                squares += some * some
    total = jnp.sum(jnp.transpose(squares), axis=0, keepdims=True)
    total = jnp.broadcast_to(total, ssend.shape)
    ssend[...] = total
    ssrecv[tp] = total
    for r in range(1, ntp):
        remote(ssend, ssrecv.at[tp], n_sem, t_peer(r)).start()
    await_recv(ssrecv, ntp - 1, n_sem)
    total = jnp.sum(ssrecv[...], axis=0)[:1]
    inverse = lax.rsqrt(total / (channels * ntp) + EPSILON)
    inverse = jnp.transpose(jnp.broadcast_to(inverse, (rows, rows)))
    for at in range(0, channels, 128):
        at = slice(at, at + 128)
        out_ref[:, at] = (gbuf[:, at] * inverse * ng_ref[:, at]).astype(BF16)

    @pl.when(seq + 1 < nseq)
    def _():
        halo.wait_send()

    await_send(drecv, nx - 1, d_sem)
    await_send(tot_recv, GROUP - 1, t_sem)
    await_send(erecv, nx - 1, e_sem)
    await_send(crecv, nx - 1, c_sem)
    for c in range(CHUNKS):
        await_send(srecv.at[c], nx - 1, s_sem.at[c])
        await_send(zrecv.at[c], GROUP - 1, zf_sem.at[c])

        @pl.when(even)
        def _():
            if c == 0:
                share_decay.wait_send()
            hand_on(c, 0, next_group).wait_send()

        if ngroups > 2:
            @pl.when(group == 1)
            def _():
                hand_on(c, 1, next_group).wait_send()
                hand_on(c, 1, after_next_group, 1).wait_send()

        await_send(szbuf.at[c], GROUP - 1, zb_sem.at[c])
        await_send(yrecv.at[c], nx - 1, y_sem.at[c])
    await_send(ssrecv, ntp - 1, n_sem)


def per_device(
    x_in, bc_in, z_in, dt_raw, starts, conv_x, conv_bc, a_log, dt_bias, d_skip, norm_gain
):
    rows, channels = x_in.shape
    state = bc_in.shape[2]
    heads = dt_raw.shape[1]
    nx, ntp = NX, lax.axis_size("tp")
    nz = lax.axis_size("seq") // nx
    width = channels // nx // CHUNKS
    total_width = channels + 2 * state
    part = state // GROUP
    operands = (
        x_in,
        bc_in,
        z_in,
        dt_raw.T,
        starts.reshape(1, rows),
        conv_x,
        conv_bc,
        a_log.reshape(1, heads),
        dt_bias.reshape(1, heads),
        d_skip.reshape(1, heads),
        norm_gain.reshape(1, channels),
    )
    operands = tuple(pltpu.with_memory_space_constraint(o, pltpu.HBM) for o in operands)
    sems = pltpu.SemaphoreType.DMA
    return pl.pallas_call(
        functools.partial(kernel, nz, nx, ntp),
        out_shape=jax.ShapeDtypeStruct((rows, channels), BF16),
        in_specs=[pl.BlockSpec(memory_space=pltpu.HBM)] * len(operands),
        out_specs=pl.BlockSpec(memory_space=pltpu.VMEM),
        scratch_shapes=[
            *(pltpu.VMEM(operand.shape, operand.dtype) for operand in operands),
            pltpu.VMEM((4 * FOLD, total_width // FOLD), BF16),
            pltpu.VMEM((4 * FOLD, total_width // FOLD), BF16),
            pltpu.VMEM((HEAD, total_width), F32),
            pltpu.VMEM((REACH + 1, total_width), F32),
            pltpu.VMEM((rows, channels), BF16),
            pltpu.VMEM((rows, channels), BF16),
            pltpu.VMEM((rows, 2 * state), BF16),
            pltpu.VMEM((nx, rows, state), BF16),
            pltpu.VMEM((nx, CHUNKS, width), F32),
            pltpu.VMEM((nx, CHUNKS, width), F32),
            pltpu.VMEM((CHUNKS, width), F32),
            pltpu.VMEM((GROUP, CHUNKS, width), F32),
            pltpu.VMEM((nx, HEAD, state + width * CHUNKS), BF16),
            pltpu.VMEM((nx, HEAD, state + width * CHUNKS), BF16),
            pltpu.VMEM((CHUNKS, nx, state, width), BF16),
            pltpu.VMEM((CHUNKS, nx, state, width), BF16),
            pltpu.VMEM((CHUNKS, nx - 1, state, width), BF16),
            pltpu.VMEM((CHUNKS, nx - 1, rows, width), F32),
            pltpu.VMEM((CHUNKS, GROUP, part, width), BF16),
            pltpu.VMEM((CHUNKS, GROUP, part, width), BF16),
            pltpu.VMEM((CHUNKS, GROUP, part, width), F32),
            pltpu.VMEM((CHUNKS, part, width), BF16),
            pltpu.VMEM((CHUNKS, 2, part, width), BF16),
            pltpu.VMEM((CHUNKS, width), F32),
            pltpu.VMEM((CHUNKS, width), F32),
            pltpu.VMEM((CHUNKS, GROUP, part, width), BF16),
            pltpu.VMEM((CHUNKS, GROUP, part, width), BF16),
            pltpu.VMEM((CHUNKS, nx, rows, width), BF16),
            pltpu.VMEM((CHUNKS, nx, rows, width), BF16),
            pltpu.VMEM((rows, channels), F32),
            pltpu.VMEM((rows, channels), F32),
            pltpu.VMEM((rows, channels), F32),
            pltpu.VMEM((rows, channels), F32),
            pltpu.VMEM((1, 128), F32),
            pltpu.VMEM((ntp, 1, 128), F32),
            sems((len(operands),)),
            sems((2,)),
            sems((2,)),
            sems((2,)),
            sems((2,)),
            sems((2,)),
            sems((CHUNKS, 2)),
            sems((CHUNKS, 2)),
            sems((CHUNKS, 4)),
            sems((2,)),
            sems((CHUNKS, 2)),
            sems((CHUNKS, 2)),
            sems((2,)),
            pltpu.SemaphoreType.REGULAR((4,)),
        ],
        compiler_params=pltpu.CompilerParams(
            collective_id=0, has_side_effects=True, vmem_limit_bytes=40 * 2**20
        ),
        cost_estimate=pl.CostEstimate(flops=2 * 10**8, bytes_accessed=2**20, transcendentals=10**6),
    )(*operands)


def solution(mesh):
    return jax.shard_map(
        per_device,
        mesh=mesh,
        in_specs=(
            P("seq", "tp"),
            P("seq", None, "tp"),
            P("seq", "tp"),
            P("seq", "tp"),
            P("seq"),
            P(None, "tp"),
            P(None, None, "tp"),
            P("tp"),
            P("tp"),
            P("tp"),
            P("tp"),
        ),
        out_specs=P("seq", "tp"),
        check_vma=False,
    )
```

```python
import functools

import jax
import jax.numpy as jnp
from jax import lax
from jax.experimental import pallas as pl
from jax.experimental.pallas import tpu as pltpu
from jax.sharding import PartitionSpec as P

NX = 4
GROUP = 4
CHUNKS = 2
HEAD = 16
REACH = 3
FOLD = 4
EPSILON = 1e-05
MESH = pl.DeviceIdType.MESH
F32, BF16 = jnp.float32, jnp.bfloat16


def dot(a, b):
    return jnp.dot(a, b, preferred_element_type=F32)


def dot_nt(a, b):
    return lax.dot_general(a, b, (((1,), (1,)), ((), ())), preferred_element_type=F32)


def dot_tn(a, b):
    return lax.dot_general(a, b, (((0,), (0,)), ((), ())), preferred_element_type=F32)


def iota(shape, axis):
    return lax.broadcasted_iota(jnp.int32, shape, axis)


def pieces(value, count):
    parts = []
    for _ in range(count):
        part = value.astype(BF16)
        parts.append(part)
        value = value - part.astype(F32)
    return jnp.concatenate(parts, axis=0)


def silu(value):
    return value * jax.nn.sigmoid(value)


def kernel(
    nz, nx, ntp,
    x_hbm, bc_hbm, z_hbm, dt_hbm, st_hbm, cx_hbm, cbc_hbm, al_hbm, db_hbm, ds_hbm, ng_hbm,
    out_ref,
    x_ref, bc_ref, z_ref, dt_ref, st_ref, cx_ref, cbc_ref, al_ref, db_ref, ds_ref, ng_ref,
    hsend, hrecv, pre, weights, xc, fx, bcv, crecv, dsend, drecv, tot_send, tot_recv,
    edge, erecv, sbuf, srecv, lbuf, ylbuf, tbuf, zrecv, prebuf, pout, pin, gsend, grecv, obuf, szbuf, ysend, yrecv,
    ebuf, yi, sz, gbuf, ssend, ssrecv,
    in_sem, h_sem, d_sem, t_sem, e_sem, c_sem, s_sem, zf_sem, p_sem, g_sem, zb_sem, y_sem, n_sem, near_sem,
):
    seq, tp = lax.axis_index("seq"), lax.axis_index("tp")
    mz, mx = seq // nx, seq % nx
    nseq, ngroups = nz * nx, nz // GROUP
    group, member = mz // GROUP, mz % GROUP
    rows, channels = x_ref.shape
    state = bc_ref.shape[2]
    heads = dt_ref.shape[0]
    quarter = channels // nx
    width = quarter // CHUNKS
    total_width = channels + 2 * state
    part = state // GROUP

    def seq_at(z, x):
        return {"seq": z * nx + x}

    def x_peer(r):
        q = (mx + r) % nx
        return q, seq_at(mz, q)

    def z_peer(r):
        k = (member + r) % GROUP
        return k, seq_at(group * GROUP + k, mx)

    def t_peer(r):
        return {"tp": (tp + r) % ntp}

    following, preceding = {"seq": seq + 1}, {"seq": seq - 1}
    swap = 1 - 2 * (member % 2)
    swapped = (group == ngroups - 1).astype(jnp.int32) * (ngroups > 2)
    to_swapped = (group == ngroups - 2).astype(jnp.int32) * (ngroups > 2)
    next_group = seq_at(mz + GROUP + to_swapped * swap, mx)

    def slice_of(k):
        return k + swapped * (1 - 2 * (k % 2))


    def remote(src, dst, sem, device):
        return pltpu.make_async_remote_copy(
            src_ref=src, dst_ref=dst, send_sem=sem.at[0], recv_sem=sem.at[1],
            device_id=device, device_id_type=MESH,
        )

    def await_recv(buffer, count, sem):
        some = buffer.at[pl.ds(0, count)]
        remote(some, some, sem, x_peer(1)[1]).wait_recv()

    def await_send(buffer, count, sem):
        some = buffer.at[pl.ds(0, count)]
        remote(some, some, sem, x_peer(1)[1]).wait_send()

    loads = [
        pltpu.make_async_copy(src, dst, in_sem.at[k])
        for k, (src, dst) in enumerate([
            (st_hbm, st_ref), (dt_hbm, dt_ref), (al_hbm, al_ref), (db_hbm, db_ref),
            (x_hbm, x_ref), (bc_hbm, bc_ref), (cx_hbm, cx_ref), (cbc_hbm, cbc_ref),
            (z_hbm, z_ref), (ds_hbm, ds_ref), (ng_hbm, ng_ref),
        ])
    ]
    for load in loads:
        load.start()

    barrier = pltpu.get_barrier_semaphore()

    def greet(device, sem=barrier):
        pl.semaphore_signal(sem, inc=1, device_id=device, device_id_type=MESH)

    for r in range(1, nx):
        greet(x_peer(r)[1])
    for r in range(1, GROUP):
        greet(z_peer(r)[1])

    first, last = member == 0, member == GROUP - 1
    below, above = group > 0, group + 1 < ngroups

    @pl.when(last & above)
    def _():
        greet(seq_at(mz + 1, mx))

    def greet_group(sem):
        for r in range(1, GROUP):
            greet(z_peer(r)[1], sem)

    @pl.when(seq > 0)
    def _():
        greet(preceding)

    for r in range(1, ntp):
        greet(t_peer(r))
    greeted = (nx - 1) + (GROUP - 1) + (ntp - 1)
    greeted += (seq + 1 < nseq).astype(jnp.int32) + (first & below).astype(jnp.int32)

    row, col = iota((rows, rows), 0), iota((rows, rows), 1)
    tril = (col <= row).astype(F32).astype(BF16)
    ranges = [tril, (col > row).astype(F32).astype(BF16)]
    for d in range(1, REACH + 1):
        ranges.append(((col <= row) & (col > row - d)).astype(F32).astype(BF16))
    spread = iota((heads, channels), 1) // (channels // heads) == iota((heads, channels), 0)
    spread = spread.astype(F32).astype(BF16)
    spread2 = jnp.concatenate([spread, spread], axis=0)
    for load in loads[:4]:
        load.wait()
    starts = jnp.broadcast_to(st_ref[...].astype(F32), (rows, rows)).astype(BF16)
    counts = dot_nt(jnp.concatenate(ranges, axis=0), starts)
    seg_col = counts[:rows]
    to_last = (counts[rows : 2 * rows] == 0.0).astype(F32)
    linked = (seg_col == dot_nt(starts, tril)) & (col <= row)
    from_first = (seg_col == 0.0).astype(F32)
    none_between = [counts[(d + 1) * rows : (d + 2) * rows] == 0.0 for d in range(1, REACH + 1)]
    taps = jnp.concatenate(
        [((col == row - d) & none_between[d - 1]).astype(F32).astype(BF16) for d in range(1, REACH + 1)],
        axis=0,
    )

    for load in loads[4:8]:
        load.wait()
    weights[:, :channels] = cx_ref[...]
    for k in range(REACH + 1):
        weights[k : k + 1, channels : channels + state] = cbc_ref[k, 0:1, :]
        weights[k : k + 1, channels + state :] = cbc_ref[k, 1:2, :]
    b_in, c_in = bc_ref[:, 0, :], bc_ref[:, 1, :]

    tail = slice(rows - 8, rows)
    last_rows = jnp.concatenate(
        [x_ref[tail, :].astype(F32), b_in[tail].astype(F32), c_in[tail].astype(F32)], axis=1
    )
    last_rows = (last_rows * to_last[tail, :1])[8 - FOLD :]
    piece = total_width // FOLD
    hsend[...] = jnp.concatenate(
        [last_rows[:, k * piece : (k + 1) * piece] for k in range(FOLD)], axis=0
    ).astype(BF16)

    def column(ref):
        square = (heads, heads)
        here = iota(square, 0) == iota(square, 1)
        return jnp.sum(jnp.where(here, jnp.broadcast_to(ref[...], square), 0.0), axis=1, keepdims=True)

    raw = dt_ref[...].astype(F32) + column(db_ref)
    step = jnp.maximum(raw, 0.0) + jnp.log1p(jnp.exp(-jnp.abs(raw)))
    decay = -jnp.exp(column(al_ref)) * step
    parts = dot_nt(pieces(decay, 3), tril)
    cumulative = parts[:heads] + parts[heads : 2 * heads] + parts[2 * heads :]
    ebuf[...] = dot_tn(pieces(jnp.exp(cumulative), 2), spread2)
    fall = ebuf[rows - 1 :, :]
    through = fall * (seg_col[rows - 1 : rows, :1] == 0.0).astype(F32)
    for q in range(nx):
        for c in range(CHUNKS):
            at = q * quarter + c * width
            dsend[q, c : c + 1, :] = through[:, at : at + width]
    factor = dot_tn(pieces(jnp.exp(-cumulative) * step, 2), spread2)

    def conv(values, at):
        size = values.shape[1]
        taken = weights[:, at : at + size]
        shifted = dot(taps, values)
        total = taken[REACH:] * values.astype(F32)
        for d in range(1, REACH + 1):
            total += taken[REACH - d : REACH - d + 1] * shifted[(d - 1) * rows : d * rows]
        pre[:, at : at + size] = total[:HEAD]
        return silu(total)

    bcv[:, :state] = conv(b_in, channels).astype(BF16)
    bcv[:, state:] = conv(c_in, channels + state).astype(BF16)
    for at in range(0, channels, 256):
        xc[:, at : at + 256] = conv(x_ref[:, at : at + 256], at).astype(BF16)

    for at in range(0, channels, 256):
        at = slice(at, at + 256)
        fx[:, at] = (xc[:, at].astype(F32) * factor[:, at]).astype(BF16)
    later = to_last * (row >= HEAD).astype(F32)
    bt = jnp.transpose(bcv[:, :state].astype(F32) * later[:, :1]).astype(BF16)
    for c in range(CHUNKS):
        for q in range(nx):
            at = slice(q * quarter + c * width, q * quarter + (c + 1) * width)
            sbuf[c, q] = (dot(bt, fx[:, at]) * fall[:, at]).astype(BF16)

    place_row, place_col = iota((HEAD, HEAD), 0), iota((HEAD, HEAD), 1)
    reached = []
    for k in range(FOLD):
        matrices = []
        for d in range(1, REACH + 1):
            here = (place_col - (k + 1) * FOLD == place_row - d) & (place_row < d)
            here &= none_between[d - 1][:HEAD, :HEAD] & (place_col >= k * FOLD)
            matrices.append(here.astype(F32).astype(BF16))
        reached.append(jnp.concatenate(matrices, axis=0))

    pl.semaphore_wait(barrier, greeted)

    halo = remote(hsend, hrecv, h_sem, following)

    @pl.when(seq + 1 < nseq)
    def _():
        halo.start()

    @pl.when(first & below)
    def _():
        greet(seq_at(mz - 1, mx), near_sem.at[0])

    for r in range(1, nx):
        q, device = x_peer(r)
        remote(dsend.at[q], drecv.at[mx], d_sem, device).start()
    def send_states(c):
        for r in (2, 1, 3) if nx == 4 else range(1, nx):
            q, device = x_peer(r)
            remote(sbuf.at[c, q], srecv.at[c, mx], s_sem.at[c], device).start()

    send_states(0)
    drecv[mx] = dsend[mx]
    for c in range(CHUNKS):
        srecv[c, mx] = sbuf[c, mx]

    @pl.when(seq == 0)
    def _():
        hrecv[...] = jnp.zeros(hrecv.shape, BF16)

    @pl.when(seq > 0)
    def _():
        halo.wait_recv()

    for k in range(FOLD):
        at = slice(k * piece, (k + 1) * piece)
        added = dot(reached[k], hrecv[...])
        total = pre[:, at]
        for d in range(1, REACH + 1):
            total += weights[REACH - d : REACH - d + 1, at] * added[(d - 1) * HEAD : d * HEAD]
        pre[:, at] = total
    done = silu(pre[...]).astype(BF16)
    xc[:HEAD, :] = done[:, :channels]
    bcv[:HEAD, :] = done[:, channels:]
    first_x = done[:, :channels].astype(F32) * factor[:HEAD]
    fx[:HEAD, :] = first_x.astype(BF16)
    first_x = (first_x * fall).astype(BF16)
    first_b = (done[:, channels : channels + state].astype(F32) * to_last[:HEAD, :1]).astype(BF16)
    for q in range(nx):
        edge[q, :, :state] = first_b
        edge[q, :, state:] = first_x[:, q * quarter : (q + 1) * quarter]
    erecv[mx] = edge[mx]
    for r in range(1, nx):
        q, device = x_peer(r)
        remote(edge.at[q], erecv.at[mx], e_sem, device).start()
    for c in range(1, CHUNKS):
        send_states(c)
    b, cc = bcv[:, :state], bcv[:, state:]
    crecv[mx] = cc

    await_recv(drecv, nx - 1, d_sem)
    reach_of = [None, drecv[0]]
    for k in range(1, nx):
        reach_of.append(reach_of[-1] * drecv[k])
    tot_send[...] = reach_of[nx]
    tot_recv[member] = reach_of[nx]
    for r in range(1, GROUP):
        k, device = z_peer(r)
        remote(tot_send, tot_recv.at[member], t_sem, device).start()
    @pl.when(last & above)
    def _():
        pl.semaphore_wait(near_sem.at[0], 1)
        greet_group(near_sem.at[1])

    scores = jnp.where(linked, dot_nt(cc, b), 0.0).astype(BF16)
    for load in loads[8:]:
        load.wait()
    skip = dot_tn(pieces(jnp.broadcast_to(column(ds_ref), (heads, 128)), 2), spread2)[:1]
    for q in range(nx):
        at = slice(q * quarter, (q + 1) * quarter)
        gate = silu(z_ref[:, at].astype(F32))
        own = ebuf[:, at] * dot(scores, fx[:, at]) + skip[:, at] * xc[:, at].astype(F32)
        yi[:, at] = own * gate
        sz[:, at] = ebuf[:, at] * from_first[:, :1] * gate

    await_recv(erecv, nx - 1, e_sem)

    def made(c, k):
        first = dot_tn(erecv[k, :, :state], erecv[k, :, state + c * width : state + (c + 1) * width])
        return srecv[c, k].astype(F32) + first

    for c in range(CHUNKS):
        await_recv(srecv.at[c], nx - 1, s_sem.at[c])
        running = made(c, 0)
        for k in range(1, nx):
            lbuf[c, k - 1] = running.astype(BF16)
            running = drecv[k, c : c + 1, :] * running + made(c, k)
        tbuf[c] = running.astype(BF16).reshape(GROUP, part, width)
        zrecv[c, member] = tbuf[c, slice_of(member)]
        for r in range(1, GROUP):
            k, device = z_peer(r)
            remote(tbuf.at[c, slice_of(k)], zrecv.at[c, member], zf_sem.at[c], device).start()

    for r in range(1, nx):
        _, device = x_peer(r)
        remote(crecv.at[mx], crecv.at[mx], c_sem, device).start()

    @pl.when(jnp.logical_not(last) & above)
    def _():
        pl.semaphore_wait(near_sem.at[1], 1)

    if ngroups > 2:
        @pl.when(first & (group == 2))
        def _():
            greet(seq_at(mz - 1, mx), near_sem.at[2])

        @pl.when(last & (group == 1))
        def _():
            pl.semaphore_wait(near_sem.at[2], 1)
            greet_group(near_sem.at[3])

    await_recv(tot_recv, GROUP - 1, t_sem)
    row_fall = [tot_recv[k] for k in range(GROUP)]
    group_fall = row_fall[0]
    for k in range(1, GROUP):
        group_fall = row_fall[k] * group_fall
    even = group % 2 == 0
    share_decay = remote(gsend, grecv, g_sem, next_group)

    def hand_on(c, slot, device, sent=0):
        return pltpu.make_async_remote_copy(
            src_ref=pout.at[c], dst_ref=pin.at[c, slot],
            send_sem=p_sem.at[c, sent], recv_sem=p_sem.at[c, 2 + slot],
            device_id=device, device_id_type=MESH,
        )

    after_next_group = seq_at(mz + 2 * GROUP + swap, mx)

    @pl.when(even)
    def _():
        gsend[...] = group_fall
        share_decay.start()
        grecv[...] = jnp.ones(grecv.shape, F32)
        pin[:, 0] = jnp.zeros((CHUNKS, part, width), BF16)

    @pl.when(group < 2)
    def _():
        pin[:, 1] = jnp.zeros((CHUNKS, part, width), BF16)

    group_totals = []
    for c in range(CHUNKS):
        await_recv(zrecv.at[c], GROUP - 1, zf_sem.at[c])
        running = zrecv[c, 0].astype(F32)
        for k in range(1, GROUP):
            prebuf[c, k] = running
            running = row_fall[k][c : c + 1] * running + zrecv[c, k].astype(F32)
        group_totals.append(running)

        @pl.when(even)
        def _():
            pout[c] = running.astype(BF16)
            hand_on(c, 0, next_group).start()

    @pl.when(jnp.logical_not(even))
    def _():
        share_decay.wait_recv()
        for c in range(CHUNKS):
            hand_on(c, 0, next_group).wait_recv()

    if ngroups > 2:
        @pl.when(group == 1)
        def _():
            @pl.when(jnp.logical_not(last))
            def _():
                pl.semaphore_wait(near_sem.at[3], 1)

            for c in range(CHUNKS):
                reached = group_fall[c : c + 1] * pin[c, 0].astype(F32) + group_totals[c]
                pout[c] = reached.astype(BF16)
                hand_on(c, 1, after_next_group, 1).start()
                hand_on(c, 1, next_group).start()

    for c in range(CHUNKS):
        if ngroups > 2:
            @pl.when(group >= 2)
            def _():
                hand_on(c, 1, next_group).wait_recv()

        before = grecv[c : c + 1] * pin[c, 1].astype(F32) + pin[c, 0].astype(F32)
        obuf[c, 0] = before.astype(BF16)
        reach = row_fall[0][c : c + 1]
        for k in range(1, GROUP):
            obuf[c, k] = (reach * before + prebuf[c, k]).astype(BF16)
            reach = row_fall[k][c : c + 1] * reach
        szbuf[c, slice_of(member)] = obuf[c, member]
        for r in range(1, GROUP):
            k, device = z_peer(r)
            remote(obuf.at[c, k], szbuf.at[c, slice_of(member)], zb_sem.at[c], device).start()

    await_recv(crecv, nx - 1, c_sem)
    for c in range(CHUNKS):
        for k in range(1, nx):
            ylbuf[c, k - 1] = dot(crecv[k], lbuf[c, k - 1])

    for c in range(CHUNKS):
        await_recv(szbuf.at[c], GROUP - 1, zb_sem.at[c])
        entering = szbuf[c].reshape(state, width)
        for k in range(nx):
            part_y = dot(crecv[k], entering)
            if k:
                part_y = reach_of[k][c : c + 1, :] * part_y + ylbuf[c, k - 1]
            ysend[c, k] = part_y.astype(BF16)
        yrecv[c, mx] = ysend[c, mx]
        for r in range(1, nx):
            q, device = x_peer(r)
            remote(ysend.at[c, q], yrecv.at[c, mx], y_sem.at[c], device).start()

    squares = jnp.zeros((rows, 128), F32)
    for c in range(CHUNKS):
        await_recv(yrecv.at[c], nx - 1, y_sem.at[c])
        for q in range(nx):
            at = slice(q * quarter + c * width, q * quarter + (c + 1) * width)
            gated = yi[:, at] + sz[:, at] * yrecv[c, q].astype(F32)
            gbuf[:, at] = gated
            for k in range(0, width, 128):
                some = gated[:, k : k + 128]
                squares += some * some
    total = jnp.sum(jnp.transpose(squares), axis=0, keepdims=True)
    total = jnp.broadcast_to(total, ssend.shape)
    ssend[...] = total
    ssrecv[tp] = total
    for r in range(1, ntp):
        remote(ssend, ssrecv.at[tp], n_sem, t_peer(r)).start()
    gbuf[...] = gbuf[...] * ng_ref[...]
    await_recv(ssrecv, ntp - 1, n_sem)
    total = jnp.sum(ssrecv[...], axis=0)[:1]
    inverse = lax.rsqrt(total / (channels * ntp) + EPSILON)
    inverse = jnp.transpose(jnp.broadcast_to(inverse, (rows, rows)))
    for at in range(0, channels, 128):
        at = slice(at, at + 128)
        out_ref[:, at] = (gbuf[:, at] * inverse).astype(BF16)

    @pl.when(seq + 1 < nseq)
    def _():
        halo.wait_send()

    await_send(drecv, nx - 1, d_sem)
    await_send(tot_recv, GROUP - 1, t_sem)
    await_send(erecv, nx - 1, e_sem)
    await_send(crecv, nx - 1, c_sem)
    for c in range(CHUNKS):
        await_send(srecv.at[c], nx - 1, s_sem.at[c])
        await_send(zrecv.at[c], GROUP - 1, zf_sem.at[c])

        @pl.when(even)
        def _():
            if c == 0:
                share_decay.wait_send()
            hand_on(c, 0, next_group).wait_send()

        if ngroups > 2:
            @pl.when(group == 1)
            def _():
                hand_on(c, 1, next_group).wait_send()
                hand_on(c, 1, after_next_group, 1).wait_send()

        await_send(szbuf.at[c], GROUP - 1, zb_sem.at[c])
        await_send(yrecv.at[c], nx - 1, y_sem.at[c])
    await_send(ssrecv, ntp - 1, n_sem)


def per_device(
    x_in, bc_in, z_in, dt_raw, starts, conv_x, conv_bc, a_log, dt_bias, d_skip, norm_gain
):
    rows, channels = x_in.shape
    state = bc_in.shape[2]
    heads = dt_raw.shape[1]
    nx, ntp = NX, lax.axis_size("tp")
    nz = lax.axis_size("seq") // nx
    width = channels // nx // CHUNKS
    total_width = channels + 2 * state
    part = state // GROUP
    operands = (
        x_in,
        bc_in,
        z_in,
        dt_raw.T,
        starts.reshape(1, rows),
        conv_x,
        conv_bc,
        a_log.reshape(1, heads),
        dt_bias.reshape(1, heads),
        d_skip.reshape(1, heads),
        norm_gain.reshape(1, channels),
    )
    operands = tuple(pltpu.with_memory_space_constraint(o, pltpu.HBM) for o in operands)
    sems = pltpu.SemaphoreType.DMA
    return pl.pallas_call(
        functools.partial(kernel, nz, nx, ntp),
        out_shape=jax.ShapeDtypeStruct((rows, channels), BF16),
        in_specs=[pl.BlockSpec(memory_space=pltpu.HBM)] * len(operands),
        out_specs=pl.BlockSpec(memory_space=pltpu.VMEM),
        scratch_shapes=[
            *(pltpu.VMEM(operand.shape, operand.dtype) for operand in operands),
            pltpu.VMEM((4 * FOLD, total_width // FOLD), BF16),
            pltpu.VMEM((4 * FOLD, total_width // FOLD), BF16),
            pltpu.VMEM((HEAD, total_width), F32),
            pltpu.VMEM((REACH + 1, total_width), F32),
            pltpu.VMEM((rows, channels), BF16),
            pltpu.VMEM((rows, channels), BF16),
            pltpu.VMEM((rows, 2 * state), BF16),
            pltpu.VMEM((nx, rows, state), BF16),
            pltpu.VMEM((nx, CHUNKS, width), F32),
            pltpu.VMEM((nx, CHUNKS, width), F32),
            pltpu.VMEM((CHUNKS, width), F32),
            pltpu.VMEM((GROUP, CHUNKS, width), F32),
            pltpu.VMEM((nx, HEAD, state + width * CHUNKS), BF16),
            pltpu.VMEM((nx, HEAD, state + width * CHUNKS), BF16),
            pltpu.VMEM((CHUNKS, nx, state, width), BF16),
            pltpu.VMEM((CHUNKS, nx, state, width), BF16),
            pltpu.VMEM((CHUNKS, nx - 1, state, width), BF16),
            pltpu.VMEM((CHUNKS, nx - 1, rows, width), F32),
            pltpu.VMEM((CHUNKS, GROUP, part, width), BF16),
            pltpu.VMEM((CHUNKS, GROUP, part, width), BF16),
            pltpu.VMEM((CHUNKS, GROUP, part, width), F32),
            pltpu.VMEM((CHUNKS, part, width), BF16),
            pltpu.VMEM((CHUNKS, 2, part, width), BF16),
            pltpu.VMEM((CHUNKS, width), F32),
            pltpu.VMEM((CHUNKS, width), F32),
            pltpu.VMEM((CHUNKS, GROUP, part, width), BF16),
            pltpu.VMEM((CHUNKS, GROUP, part, width), BF16),
            pltpu.VMEM((CHUNKS, nx, rows, width), BF16),
            pltpu.VMEM((CHUNKS, nx, rows, width), BF16),
            pltpu.VMEM((rows, channels), F32),
            pltpu.VMEM((rows, channels), F32),
            pltpu.VMEM((rows, channels), F32),
            pltpu.VMEM((rows, channels), F32),
            pltpu.VMEM((1, 128), F32),
            pltpu.VMEM((ntp, 1, 128), F32),
            sems((len(operands),)),
            sems((2,)),
            sems((2,)),
            sems((2,)),
            sems((2,)),
            sems((2,)),
            sems((CHUNKS, 2)),
            sems((CHUNKS, 2)),
            sems((CHUNKS, 4)),
            sems((2,)),
            sems((CHUNKS, 2)),
            sems((CHUNKS, 2)),
            sems((2,)),
            pltpu.SemaphoreType.REGULAR((4,)),
        ],
        compiler_params=pltpu.CompilerParams(
            collective_id=0, has_side_effects=True, vmem_limit_bytes=40 * 2**20
        ),
        cost_estimate=pl.CostEstimate(flops=2 * 10**8, bytes_accessed=2**20, transcendentals=10**6),
    )(*operands)


def solution(mesh):
    return jax.shard_map(
        per_device,
        mesh=mesh,
        in_specs=(
            P("seq", "tp"),
            P("seq", None, "tp"),
            P("seq", "tp"),
            P("seq", "tp"),
            P("seq"),
            P(None, "tp"),
            P(None, None, "tp"),
            P("tp"),
            P("tp"),
            P("tp"),
            P("tp"),
        ),
        out_specs=P("seq", "tp"),
        check_vma=False,
    )
```
